256 devices in a mesh: space: 64 (over x, y, z_lo, core), tm: 4 (over z_hi).
Axes of the slice: x: 4, y: 4, z: 8 (z_hi: 4, z_lo: 2; z = z_hi * 2 + z_lo), core: 2. Of those that a mesh axis runs over, the one named last changes fastest.
Arguments:
- snapshots: bfloat16 [2048, 3, 49152], P('tm', None, 'space'), may hold values from -15 to 15
- tail: bfloat16 [64, 3, 49152], P(None, None, 'space'), may hold values from -15 to 15
- volume: float32 [49152], P('space'), may hold values from 0.3 to 3
Outputs:
- gram: float32 [64, 2, 32, 32], P('tm')
- modes: bfloat16 [64, 2, 32, 3, 49152], P('tm', None, None, None, 'space')
The draws below stay inside these ranges and needn't reach their ends.
All inputs are finite; a program needn't handle non-finite values.
Results may differ from the reference program's by a relative error of at most 0.00055.
The reference program's roundings to bfloat16 on the way count: a program that leaves them out, or rounds other values in their place, can miss the bound.
Values may be sent and summed in bfloat16 or wider, within the bound.
No kernel may reach another device: no remote copies, remote signals or barrier semaphores. Data moves between devices by JAX's collectives and lax.ppermute only.
A program may use at most 128 MiB of HBM per device.

```python
import math
import jax
import jax.numpy as jnp
from jax import lax

PDEV = 768
NB = 32
NFFT = 128
HOP = 64
SLOTS = 64
NPOINTS = 49152


def wave_field(key, start, count):
    keys = jax.random.split(jax.random.fold_in(key, 11), 6)
    waves = 3
    rates = 2.0 * jnp.pi * jax.random.uniform(keys[0], (waves,), jnp.float32, 3.0, 40.0) / NFFT
    amps = jax.random.uniform(keys[1], (waves, 3, NPOINTS), jnp.float32, -1.0, 1.0)
    phases = jax.random.uniform(keys[2], (waves, 3, NPOINTS), jnp.float32, -jnp.pi, jnp.pi)
    scale = jnp.exp(jax.random.uniform(keys[3], (NPOINTS,), jnp.float32, jnp.log(0.3), jnp.log(3.0)))
    drift = jax.random.uniform(keys[4], (waves,), jnp.float32, 0.0, 2.0 * jnp.pi)
    slow = 2.0 * jnp.pi * jax.random.uniform(keys[5], (waves,), jnp.float32, 1.0, 4.0) / (NB * HOP)
    times = start + jnp.arange(count, dtype=jnp.float32)
    field = jnp.zeros((count, 3, NPOINTS), jnp.float32)
    for wave in range(waves):
        envelope = 1.0 + 0.5 * jnp.sin(slow[wave] * times + drift[wave])
        field = field + envelope[:, None, None] * amps[wave] * jnp.cos(rates[wave] * times[:, None, None] + phases[wave])
    return field * scale


def noise_field(key, count):
    return jnp.clip(0.4 * jax.random.normal(key, (count, 3, NPOINTS), jnp.float32), -1.0, 1.0)


def draw_snapshots(key, part):
    field = wave_field(key, 0.0, NB * HOP)
    key = jax.random.fold_in(key, 3)
    return (field + noise_field(key, NB * HOP)).astype(jnp.bfloat16)


def draw_tail(key, part):
    field = wave_field(key, 1.0 * NB * HOP, HOP)
    key = jax.random.fold_in(key, 5)
    return (field + noise_field(key, HOP)).astype(jnp.bfloat16)


def block_levels(own_key, shape, shards, smallest, largest):
    level = 1.0
    for axis_at, blocks in shards:
        draws = jax.random.uniform(jax.random.fold_in(jax.random.fold_in(own_key, 6), axis_at), (blocks,), jnp.float32, smallest / len(shards), largest / len(shards))
        level = level * jnp.repeat(jnp.exp(draws), shape[axis_at] // blocks).reshape((-1,) + (1,) * (len(shape) - 1 - axis_at))
    return level


def setup_inputs(seed: int = 0) -> dict:
    key_list = jax.random.split(jax.random.key(seed), 4)
    return {
        "snapshots": draw_snapshots(jax.random.fold_in(key_list[3], 71), 0),
        "tail": draw_tail(jax.random.fold_in(key_list[3], 71), 0),
        "volume": jnp.clip(jnp.exp(math.log(3.0) - 2.3025851 * jax.random.uniform(key_list[2], (NPOINTS,), jnp.float32) ** block_levels(key_list[2], (NPOINTS,), ((0, 64),), -0.2, 0.2)), 0.3, 3.0),
    }


def transform_table():
    times = jnp.arange(NFFT, dtype=jnp.float32)
    freq = jnp.arange(NFFT // 2, dtype=jnp.float32)[:, None]
    window = 0.5 - 0.5 * jnp.cos(2.0 * jnp.pi * times / NFFT)
    window = window / jnp.sqrt(jnp.sum(window * window))
    angles = 2.0 * jnp.pi * freq * times[None, :] / NFFT
    real_rows = window * jnp.cos(angles)
    imag_rows = -window * jnp.sin(angles)
    nyquist = window * jnp.cos(jnp.pi * times)
    imag_rows = jnp.where(freq == 0.0, nyquist[None, :], imag_rows)
    return jnp.stack([real_rows, imag_rows], axis=1).reshape(NFFT, NFFT).astype(jnp.bfloat16)

def assemble(total, first_slot):
    count = total.shape[0]
    is_zero = (first_slot + jnp.arange(count, dtype=jnp.int32) == 0)[:, None, None]
    gram_real = total[:, 0] + total[:, 1]
    gram_imag = total[:, 2] - jnp.swapaxes(total[:, 2], 1, 2)
    mat_a = jnp.where(is_zero, total[:, 0], gram_real)
    mat_b = jnp.where(is_zero, total[:, 1], gram_real)
    mat_i = jnp.where(is_zero, jnp.zeros_like(gram_imag), gram_imag)
    gram = jnp.stack([mat_a, jnp.where(is_zero, total[:, 1], gram_imag)], axis=1)
    norm_a = jnp.sqrt(lax.optimization_barrier(jnp.sum(mat_a * mat_a + mat_i * mat_i, axis=(1, 2))) + 1e-06)[:, None, None]
    norm_b = jnp.sqrt(lax.optimization_barrier(jnp.sum(mat_b * mat_b + mat_i * mat_i, axis=(1, 2))) + 1e-06)[:, None, None]
    scaled = ((mat_a / norm_a).astype(jnp.bfloat16), (mat_i / norm_a).astype(jnp.bfloat16), (mat_b / norm_b).astype(jnp.bfloat16), (mat_i / norm_b).astype(jnp.bfloat16))
    return (gram, scaled)

def project(scaled, real_part, imag_part):
    ga, gia, gb, gib = [m.astype(jnp.float32) for m in scaled]
    re32 = real_part.astype(jnp.float32)
    im32 = imag_part.astype(jnp.float32)
    first = jnp.einsum('skj,jsx->skx', ga, re32) + jnp.einsum('skj,jsx->skx', gia, im32)
    second = jnp.einsum('skj,jsx->skx', gb, im32) - jnp.einsum('skj,jsx->skx', gib, re32)
    return jnp.stack([first, second], axis=1).astype(jnp.bfloat16)

def reference(snapshots, tail, volume):
    table = transform_table().astype(jnp.float32)
    npoints = snapshots.shape[2]
    count = npoints // PDEV
    spec_buf = jnp.zeros((NB, NFFT, 3, npoints), jnp.bfloat16)
    acc = jnp.zeros((SLOTS, 3, NB, NB), jnp.float32)

    def first_pass(index, carry):
        buf, total = carry
        start = (index * PDEV).astype(jnp.int32)
        data = lax.dynamic_slice_in_dim(snapshots, start, PDEV, 2)
        tail_part = lax.dynamic_slice_in_dim(tail, start, PDEV, 2)
        halves = jnp.concatenate([data, tail_part], 0).reshape(NB + 1, HOP, 3 * PDEV).astype(jnp.float32)
        spec = (jnp.einsum('rt,htx->hrx', table[:, :HOP], halves[:-1]) + jnp.einsum('rt,htx->hrx', table[:, HOP:], halves[1:])).astype(jnp.bfloat16)
        weights = jnp.tile(lax.dynamic_slice_in_dim(volume, start, PDEV, 0), 3)
        parts = spec.reshape(NB, SLOTS, 2, 3 * PDEV)
        real_part = parts[:, :, 0]
        imag_part = parts[:, :, 1]
        w_real = (real_part * weights).astype(jnp.bfloat16).astype(jnp.float32)
        w_imag = (imag_part * weights).astype(jnp.bfloat16).astype(jnp.float32)
        re32 = real_part.astype(jnp.float32)
        im32 = imag_part.astype(jnp.float32)
        terms = jnp.stack([jnp.einsum('isx,jsx->sij', w_real, re32), jnp.einsum('isx,jsx->sij', w_imag, im32), jnp.einsum('isx,jsx->sij', w_real, im32)], axis=1)
        buf = lax.dynamic_update_slice_in_dim(buf, spec.reshape(NB, NFFT, 3, PDEV), start, 3)
        return (buf, total + terms)
    spec_buf, acc = lax.fori_loop(0, count, first_pass, (spec_buf, acc))
    total = acc / (NB * 3 * npoints)
    gram, scaled = assemble(total, 0)
    modes = jnp.zeros((SLOTS, 2, NB, 3, npoints), jnp.bfloat16)

    def second_pass(index, buf):
        start = (index * PDEV).astype(jnp.int32)
        spec = lax.dynamic_slice_in_dim(spec_buf, start, PDEV, 3)
        parts = spec.reshape(NB, SLOTS, 2, 3 * PDEV)
        out = project(scaled, parts[:, :, 0], parts[:, :, 1]).reshape(SLOTS, 2, NB, 3, PDEV)
        return lax.dynamic_update_slice_in_dim(buf, out, start, 4)
    modes = lax.fori_loop(0, count, second_pass, modes)
    return (gram, modes)
```

```python
import functools

import jax
import jax.numpy as jnp
import ml_dtypes
import numpy as np
from jax import lax
from jax.experimental import pallas as pl
from jax.experimental.pallas import tpu as pltpu
from jax.sharding import PartitionSpec as P

NB = 32
NFFT = 128
HOP = 64
SLOTS = 64
PDEV = 768
NPOINTS = 49152
TM = 4
OWN = NB // TM
HERE = SLOTS // TM
SPAN = OWN * HOP
CHUNKS = (6, 6, 4)
F32, BF16 = jnp.float32, jnp.bfloat16


def transform_table():
    times = np.arange(NFFT)
    freq = np.arange(SLOTS)[:, None]
    window = 0.5 - 0.5 * np.cos(2.0 * np.pi * times / NFFT)
    window = window / np.sqrt(np.sum(window * window))
    angles = 2.0 * np.pi * ((freq * times[None, :]) % NFFT) / NFFT
    real_rows = window * np.cos(angles)
    imag_rows = -window * np.sin(angles)
    nyquist = window * np.cos(np.pi * times)
    imag_rows = np.where(freq == 0, nyquist[None, :], imag_rows)
    return np.stack([real_rows, imag_rows], axis=1).astype(ml_dtypes.bfloat16)


def banded_table():
    table = transform_table()
    band = np.zeros((SLOTS, 2, OWN, SPAN + HOP), ml_dtypes.bfloat16)
    for b in range(OWN):
        band[:, :, b, b * HOP : b * HOP + NFFT] = table
    return band.reshape(TM, HERE, 2 * OWN, SPAN + HOP)


def transform_kernel(band, snaps, follow, tail, *outs):
    rank = lax.axis_index("tm")
    own = snaps[0]
    last = (rank == TM - 1).astype(jnp.int32)
    pick = jnp.full((HOP, PDEV), last, jnp.int32) > 0
    next_half = jnp.where(pick, tail[0].astype(F32), follow[0].astype(F32)).astype(BF16)
    for k, out in enumerate(outs):
        rows = band[(rank + k) % TM]
        got = jnp.dot(rows[:, :SPAN], own, preferred_element_type=F32)
        got += jnp.dot(rows[:, SPAN:], next_half, preferred_element_type=F32)
        out[:, 0] = got.reshape(out.shape[0], 2 * OWN, PDEV).astype(BF16)


def transform(band, snaps, follow, tail):
    count = band.shape[1]
    rows = jnp.asarray(band.reshape(TM, count * 2 * OWN, SPAN + HOP))
    return pl.pallas_call(
        transform_kernel,
        grid=(3,),
        in_specs=[
            pl.BlockSpec(rows.shape, lambda c: (0, 0, 0)),
            pl.BlockSpec((1, SPAN, PDEV), lambda c: (c, 0, 0)),
            pl.BlockSpec((1, HOP, PDEV), lambda c: (c, 0, 0)),
            pl.BlockSpec((1, HOP, PDEV), lambda c: (c, 0, 0)),
        ],
        out_specs=[pl.BlockSpec((count, 1, 2 * OWN, PDEV), lambda c: (0, c, 0, 0))] * TM,
        out_shape=[jax.ShapeDtypeStruct((count, 3, 2 * OWN, PDEV), BF16)] * TM,
        compiler_params=pltpu.CompilerParams(vmem_limit_bytes=32 << 20),
        cost_estimate=pl.CostEstimate(
            flops=2 * TM * count * 16 * 576 * 3 * PDEV, bytes_accessed=8 << 20, transcendentals=0
        ),
        name="transform",
    )(rows, snaps, follow, tail)


def zero_lanes(first_pair):
    is_zero = (lax.axis_index("tm") == 0) & (pl.program_id(0) + first_pair == 0)
    return jnp.where(is_zero, 2 * NB, 0)


def gram_kernel(first_pair, own, behind1, behind2, behind3, volume, terms, spec, held):
    rank = lax.axis_index("tm")
    for k, piece in enumerate((own, behind1, behind2, behind3)):
        held[(rank + TM - k) % TM] = piece[...]
    weights = volume[...]
    total = jnp.zeros((4 * NB, 4 * NB), F32)
    for c in range(3):
        rows = []
        for s in range(2):
            pieces = [held[q, s, c].astype(F32) for q in range(TM)]
            rows += [p[:OWN] for p in pieces] + [p[OWN:] for p in pieces]
        both = jnp.concatenate(rows, 0)
        plain = both.astype(BF16)
        weighted = (both * weights).astype(BF16)
        spec[0, c] = plain
        total += lax.dot_general(
            weighted, plain, (((1,), (1,)), ((), ())), preferred_element_type=F32
        )
    lane = lax.broadcasted_iota(jnp.int32, (NB, 4 * NB), 1)
    first, low = lane < 2 * NB, (lane % (2 * NB)) < NB
    top = jnp.where(first, total[:NB], total[2 * NB : 3 * NB])
    bottom = jnp.where(first, total[NB : 2 * NB], total[3 * NB :])
    summed = top + jnp.where(low, pltpu.roll(bottom, 3 * NB, 1), 0.0)
    apart = jnp.where(lane < NB, top, bottom)
    terms[0] = jnp.where(lane < zero_lanes(first_pair), apart, summed)


def gram_terms(first_pair, pieces, volume):
    pairs = pieces[0].shape[0] // 2
    piece = pl.BlockSpec((2, 3, 2 * OWN, PDEV), lambda p: (p, 0, 0, 0))
    return pl.pallas_call(
        functools.partial(gram_kernel, first_pair),
        grid=(pairs,),
        in_specs=[piece] * TM + [pl.BlockSpec((1, PDEV), lambda p: (0, 0))],
        out_specs=[
            pl.BlockSpec((1, NB, 4 * NB), lambda p: (p, 0, 0)),
            pl.BlockSpec((1, 3, 4 * NB, PDEV), lambda p: (p, 0, 0, 0)),
        ],
        out_shape=[
            jax.ShapeDtypeStruct((pairs, NB, 4 * NB), F32),
            jax.ShapeDtypeStruct((pairs, 3, 4 * NB, PDEV), BF16),
        ],
        scratch_shapes=[pltpu.VMEM((TM, 2, 3, 2 * OWN, PDEV), BF16)],
        compiler_params=pltpu.CompilerParams(vmem_limit_bytes=32 << 20),
        cost_estimate=pl.CostEstimate(
            flops=pairs * 2 * 128 * 128 * 3 * PDEV,
            bytes_accessed=pairs * 4 * 3 * 128 * PDEV,
            transcendentals=0,
        ),
        name="gram_terms",
    )(*pieces, volume)


def modes_kernel(first_pair, t0, t1, t2, t3, spec, *rest):
    gram, modes = rest[-2:]
    total = ((t0[0] + t1[0]) + (t2[0] + t3[0])) / (NB * 3 * NPOINTS)
    lane = lax.broadcasted_iota(jnp.int32, (NB, 4 * NB), 1)
    first, low = lane < 2 * NB, (lane % (2 * NB)) < NB
    zero = lane < zero_lanes(first_pair)
    flipped = jnp.concatenate([total] * 4, 0).T
    cross_t = jnp.where(first, flipped[NB : 2 * NB], flipped[3 * NB :])
    mat = jnp.where(low, total, jnp.where(zero, total, total - cross_t))
    for s in range(2):
        for part in range(2):
            at = (2 * s + part) * NB
            gram[s, part] = mat[:, at : at + NB]
    squares = mat * mat

    def part_sum(keep):
        return jnp.sum(jnp.where(keep, squares, 0.0), keepdims=True)

    e0, e1 = part_sum(lane < NB), part_sum(first & ~low)
    rest_sum = part_sum(~first)
    zero_here = zero[:1, :1]
    norm_a = jnp.sqrt(jnp.where(zero_here, e0, e0 + e1) + 1e-06)
    norm_b = jnp.sqrt(jnp.where(zero_here, e1, e0 + e1) + 1e-06)
    norm_rest = jnp.sqrt(rest_sum + 1e-06)
    turned = jnp.where(low, -pltpu.roll(mat, 3 * NB, 1), pltpu.roll(mat, NB, 1))
    part_a = jnp.where(zero, jnp.where(low, mat, 0.0), mat)
    part_b = jnp.where(zero, jnp.where(low, 0.0, mat), turned)
    part_a = part_a / jnp.where(first, norm_a, norm_rest)
    part_b = part_b / jnp.where(first, norm_b, norm_rest)
    mixing = jnp.concatenate(
        [
            jnp.where(first, part_a, 0.0),
            jnp.where(first, part_b, 0.0),
            jnp.where(first, 0.0, part_a),
            jnp.where(first, 0.0, part_b),
        ],
        0,
    ).astype(BF16)
    for c in range(3):
        got = jnp.dot(mixing, spec[0, c], preferred_element_type=F32)
        modes[:, :, c] = got.reshape(2, 2, NB, PDEV).astype(BF16)


def project(first_pair, totals, spec, before):
    pairs = spec.shape[0]
    term = pl.BlockSpec((1, NB, 4 * NB), lambda p: (p, 0, 0))
    return pl.pallas_call(
        functools.partial(modes_kernel, first_pair),
        grid=(pairs,),
        in_specs=[term] * 4
        + [pl.BlockSpec((1, 3, 4 * NB, PDEV), lambda p: (p, 0, 0, 0))]
        + [pl.BlockSpec(memory_space=pl.ANY)] * len(before),
        out_specs=[
            pl.BlockSpec((2, 2, NB, NB), lambda p: (p + first_pair, 0, 0, 0)),
            pl.BlockSpec((2, 2, 3, NB, PDEV), lambda p: (p + first_pair, 0, 0, 0, 0)),
        ],
        out_shape=[
            jax.ShapeDtypeStruct((HERE, 2, NB, NB), F32),
            jax.ShapeDtypeStruct((HERE, 2, 3, NB, PDEV), BF16),
        ],
        input_output_aliases={5 + i: i for i in range(len(before))},
        compiler_params=pltpu.CompilerParams(vmem_limit_bytes=32 << 20),
        cost_estimate=pl.CostEstimate(
            flops=pairs * 2 * 128 * 128 * 3 * PDEV,
            bytes_accessed=pairs * 4 * 3 * 128 * PDEV,
            transcendentals=0,
        ),
        name="modes",
    )(*totals, spec, *before)


def over_space(block, mask):
    route = [(i, i ^ mask) for i in range(lax.axis_size("space"))]
    return lax.ppermute(block, "space", route)


def from_behind(block, distance):
    route = [(i, (i + distance) % TM) for i in range(TM)]
    return lax.ppermute(block, "tm", route)


def sum_over_space(terms):
    for shift in (4, 2, 0):
        got = [terms] + [over_space(terms, m << shift) for m in (1, 2, 3)]
        if shift:
            terms = (got[0] + got[1]) + (got[2] + got[3])
    return got


def body(snapshots, tail, volume):
    snaps = jnp.transpose(snapshots, (1, 0, 2))
    tail = jnp.transpose(tail, (1, 0, 2))
    weights = volume.reshape(1, PDEV)
    follow = lax.ppermute(snaps[:, :HOP], "tm", [(i, i - 1) for i in range(1, TM)])
    band = banded_table()
    start = 0
    done = ()
    sent = []
    for count in CHUNKS:
        pieces = transform(band[:, start : start + count], snaps, follow, tail)
        sent.append([pieces[0]] + [from_behind(pieces[k], k) for k in range(1, TM)])
        start += count
    start = 0
    for count, pieces in zip(CHUNKS, sent):
        terms, spec = gram_terms(start // 2, pieces, weights)
        done = project(start // 2, sum_over_space(terms), spec, done)
        start += count
    gram, modes = done
    return gram, jnp.transpose(modes, (0, 1, 3, 2, 4))


def solution(mesh):
    placed = (P("tm", None, "space"), P(None, None, "space"), P("space"))
    return jax.shard_map(
        body,
        mesh=mesh,
        in_specs=placed,
        out_specs=(P("tm", None, None, None), P("tm", None, None, None, "space")),
        check_vma=False,
    )
```

```python
import functools

import jax
import jax.numpy as jnp
import ml_dtypes
import numpy as np
from jax import lax
from jax.experimental import pallas as pl
from jax.experimental.pallas import tpu as pltpu
from jax.sharding import PartitionSpec as P

NB = 32
NFFT = 128
HOP = 64
SLOTS = 64
PDEV = 768
NPOINTS = 49152
TM = 4
OWN = NB // TM
HALF = OWN // 2
HERE = SLOTS // TM
BODY = HALF * HOP
ALL = (0, HERE // 2)
LONG = 10**12
F32, BF16 = jnp.float32, jnp.bfloat16
ANY = pl.BlockSpec(memory_space=pl.ANY)
WHOLE, PART = 60 << 20, 16 << 20


def transform_table():
    f32 = np.float32
    times = np.arange(NFFT, dtype=f32)
    freq = np.arange(SLOTS, dtype=f32)[:, None]
    window = f32(0.5) - f32(0.5) * np.cos(f32(2.0 * np.pi) * times / f32(NFFT))
    window = window / np.sqrt(np.sum(window * window))
    angles = f32(2.0 * np.pi) * freq * times[None, :] / f32(NFFT)
    real_rows = window * np.cos(angles)
    imag_rows = -window * np.sin(angles)
    nyquist = window * np.cos(f32(np.pi) * times)
    imag_rows = np.where(freq == 0, nyquist[None, :], imag_rows)
    return np.stack([real_rows, imag_rows], axis=1).astype(ml_dtypes.bfloat16)


def banded_table():
    table = transform_table()
    band = np.zeros((SLOTS, 2, HALF, BODY + HOP), ml_dtypes.bfloat16)
    for b in range(HALF):
        band[:, :, b, b * HOP : b * HOP + NFFT] = table
    return band.reshape(TM, HERE * 2 * HALF, BODY + HOP)


def transform_kernel(pairs, late, band, main, *rest):
    rank = lax.axis_index("tm")
    if late:
        outs = rest[2:]
        follow, tail = rest[:2]
        last = (rank == TM - 1).astype(jnp.int32)
        pick = jnp.full((HOP, PDEV), last, jnp.int32) > 0
        after = jnp.where(pick, tail[0].astype(F32), follow[0].astype(F32)).astype(BF16)
    else:
        outs = rest[1:]
        after = rest[0][0]
    first, stop = (4 * HALF * p for p in pairs)
    rows = jnp.concatenate([band[(rank + k) % TM, first:stop] for k in range(TM)], 0)
    got = jnp.dot(rows[:, :BODY], main[0], preferred_element_type=F32)
    got += jnp.dot(rows[:, BODY:], after, preferred_element_type=F32)
    got = got.astype(BF16).reshape(TM, pairs[1] - pairs[0], 4 * HALF, PDEV)
    for k, out in enumerate(outs[:TM]):
        out[:, 0] = got[k]
    if len(outs) > TM:
        outs[TM][...] = main[:, :HOP]


def transform(band, snaps, pairs, half, ends=(), edge=False):
    count = pairs[1] - pairs[0]
    piece = jax.ShapeDtypeStruct((count, 3, 4 * HALF, PDEV), BF16)
    strip = jax.ShapeDtypeStruct((3, HOP, PDEV), BF16)
    if half:
        ends_specs = [pl.BlockSpec((1, HOP, PDEV), lambda c: (c, 0, 0))] * 2
    else:
        ends, ends_specs = (snaps,), [pl.BlockSpec((1, HOP, PDEV), lambda c: (c, HALF, 0))]
    return pl.pallas_call(
        functools.partial(transform_kernel, pairs, half),
        grid=(3,),
        in_specs=[
            pl.BlockSpec(band.shape, lambda c: (0, 0, 0)),
            pl.BlockSpec((1, BODY, PDEV), lambda c: (c, half, 0)),
        ]
        + ends_specs,
        out_specs=[pl.BlockSpec((count, 1, 4 * HALF, PDEV), lambda c: (0, c, 0, 0))] * TM
        + [pl.BlockSpec((1, HOP, PDEV), lambda c: (c, 0, 0))] * edge,
        out_shape=[piece] * TM + [strip] * edge,
        compiler_params=pltpu.CompilerParams(vmem_limit_bytes=PART if half else WHOLE),
        cost_estimate=pl.CostEstimate(flops=LONG, bytes_accessed=0, transcendentals=0),
        name="transform",
    )(band, snaps, *ends)


def zero_lanes(first_pair, pair):
    is_zero = (lax.axis_index("tm") == 0) & (pair + first_pair == 0)
    return jnp.where(is_zero, 2 * NB, 0)


def lane_masks():
    lane = lax.broadcasted_iota(jnp.int32, (NB, 4 * NB), 1)
    return lane, lane < 2 * NB, (lane % (2 * NB)) < NB


def gram_kernel(first_pair, *refs):
    early, late, volume = refs[:TM], refs[TM : 2 * TM], refs[2 * TM]
    terms, spec, held = refs[-3:]
    rank = lax.axis_index("tm")
    for k in range(TM):
        held[(rank + TM - k) % TM, 0] = early[k][0]
        held[(rank + TM - k) % TM, 1] = late[k][0]
    weights = volume[...]
    upper = lax.broadcasted_iota(jnp.int32, (OWN, PDEV), 0) < HALF
    total = jnp.zeros((4 * NB, 4 * NB), F32)
    for c in range(3):
        rows = []
        for s in range(2):
            real, imag = [], []
            for q in range(TM):
                a = held[q, 0, c].astype(F32)[s * OWN : (s + 1) * OWN]
                b = held[q, 1, c].astype(F32)[s * OWN : (s + 1) * OWN]
                real.append(jnp.where(upper, a, pltpu.roll(b, HALF, 0)))
                imag.append(jnp.where(upper, pltpu.roll(a, HALF, 0), b))
            rows += real + imag
        both = jnp.concatenate(rows, 0)
        plain = both.astype(BF16)
        weighted = (both * weights).astype(BF16)
        spec[0, c] = plain
        total += lax.dot_general(
            weighted, plain, (((1,), (1,)), ((), ())), preferred_element_type=F32
        )
    lane, first, low = lane_masks()
    top = jnp.where(first, total[:NB], total[2 * NB : 3 * NB])
    bottom = jnp.where(first, total[NB : 2 * NB], total[3 * NB :])
    summed = top + jnp.where(low, pltpu.roll(bottom, 3 * NB, 1), 0.0)
    apart = jnp.where(lane < NB, top, bottom)
    terms[0] = jnp.where(lane < zero_lanes(first_pair, pl.program_id(0)), apart, summed)


def gram_terms(group, pairs, early, late, volume, before=(), wait=(), cost=0):
    count = pairs[1] - pairs[0]
    skip = pairs[0] - group[0]
    size = group[1] - group[0]
    late_piece = pl.BlockSpec((1, 3, 4 * HALF, PDEV), lambda p: (p, 0, 0, 0))
    early_piece = pl.BlockSpec((1, 3, 4 * HALF, PDEV), lambda p: (p + skip, 0, 0, 0))
    return pl.pallas_call(
        functools.partial(gram_kernel, pairs[0]),
        grid=(count,),
        in_specs=[early_piece] * TM
        + [late_piece] * TM
        + [pl.BlockSpec((1, PDEV), lambda p: (0, 0))]
        + [ANY] * (len(before) + len(wait)),
        out_specs=[
            pl.BlockSpec((1, NB, 4 * NB), lambda p: (p + skip, 0, 0)),
            pl.BlockSpec((1, 3, 4 * NB, PDEV), lambda p: (p + skip, 0, 0, 0)),
        ],
        out_shape=[
            jax.ShapeDtypeStruct((size, NB, 4 * NB), F32),
            jax.ShapeDtypeStruct((size, 3, 4 * NB, PDEV), BF16),
        ],
        scratch_shapes=[pltpu.VMEM((TM, 2, 3, 4 * HALF, PDEV), BF16)],
        input_output_aliases={2 * TM + 1 + i: i for i in range(len(before))},
        compiler_params=pltpu.CompilerParams(vmem_limit_bytes=PART),
        cost_estimate=pl.CostEstimate(flops=cost, bytes_accessed=0, transcendentals=0),
        name="gram_terms",
    )(*early, *late, volume, *before, *wait)


def mix(first_pair, pair, total):
    lane, first, low = lane_masks()
    zero = lane < zero_lanes(first_pair, pair)
    flipped = jnp.concatenate([total] * 4, 0).T
    cross_t = jnp.where(first, flipped[NB : 2 * NB], flipped[3 * NB :])
    mat = jnp.where(low, total, jnp.where(zero, total, total - cross_t))
    squares = mat * mat

    def part_sum(keep):
        return jnp.sum(jnp.where(keep, squares, 0.0), keepdims=True)

    e0, e1 = part_sum(lane < NB), part_sum(first & ~low)
    rest_sum = part_sum(~first)
    zero_here = zero[:1, :1]
    norm_a = jnp.sqrt(jnp.where(zero_here, e0, e0 + e1) + 1e-06)
    norm_b = jnp.sqrt(jnp.where(zero_here, e1, e0 + e1) + 1e-06)
    norm_rest = jnp.sqrt(rest_sum + 1e-06)
    turned = jnp.where(low, -pltpu.roll(mat, 3 * NB, 1), pltpu.roll(mat, NB, 1))
    part_a = jnp.where(zero, jnp.where(low, mat, 0.0), mat)
    part_b = jnp.where(zero, jnp.where(low, 0.0, mat), turned)
    part_a = part_a / jnp.where(first, norm_a, norm_rest)
    part_b = part_b / jnp.where(first, norm_b, norm_rest)
    mixing = jnp.concatenate(
        [
            jnp.where(first, part_a, 0.0),
            jnp.where(first, part_b, 0.0),
            jnp.where(first, 0.0, part_a),
            jnp.where(first, 0.0, part_b),
        ],
        0,
    )
    return mat, mixing.astype(BF16)


def modes_kernel(pairs, t0, t1, t2, t3, spec, *rest):
    gram, modes, mats, mixings = rest[-4:]
    pair = pl.program_id(0)

    @pl.when(pair == 0)
    def _():
        for p in range(pairs[1] - pairs[0]):
            total = ((t0[p] + t1[p]) + (t2[p] + t3[p])) / (NB * 3 * NPOINTS)
            mats[p], mixings[p] = mix(pairs[0], p, total)

    mat = mats[pair]
    for s in range(2):
        for part in range(2):
            at = (2 * s + part) * NB
            gram[s, part] = mat[:, at : at + NB]
    for c in range(3):
        got = jnp.dot(mixings[pair], spec[0, c], preferred_element_type=F32)
        modes[:, :, c] = got.astype(BF16).reshape(2, 2, NB, PDEV)


def project(pairs, totals, spec, before):
    first, count = pairs[0], pairs[1] - pairs[0]
    return pl.pallas_call(
        functools.partial(modes_kernel, pairs),
        grid=(count,),
        in_specs=[pl.BlockSpec((count, NB, 4 * NB), lambda p: (0, 0, 0))] * 4
        + [pl.BlockSpec((1, 3, 4 * NB, PDEV), lambda p: (p, 0, 0, 0))]
        + [ANY] * len(before),
        out_specs=[
            pl.BlockSpec((2, 2, NB, NB), lambda p: (p + first, 0, 0, 0)),
            pl.BlockSpec((2, 2, 3, NB, PDEV), lambda p: (p + first, 0, 0, 0, 0)),
        ],
        out_shape=[
            jax.ShapeDtypeStruct((HERE, 2, NB, NB), F32),
            jax.ShapeDtypeStruct((HERE, 2, 3, NB, PDEV), BF16),
        ],
        scratch_shapes=[
            pltpu.VMEM((count, NB, 4 * NB), F32),
            pltpu.VMEM((count, 4 * NB, 4 * NB), BF16),
        ],
        input_output_aliases={5 + i: i for i in range(len(before))},
        compiler_params=pltpu.CompilerParams(vmem_limit_bytes=PART),
        cost_estimate=pl.CostEstimate(flops=0, bytes_accessed=0, transcendentals=0),
        name="modes",
    )(*totals, spec, *before)


def over_space(block, mask):
    route = [(i, i ^ mask) for i in range(lax.axis_size("space"))]
    return lax.ppermute(block, "space", route)


def from_behind(block, distance):
    route = [(i, (i + distance) % TM) for i in range(TM)]
    return lax.ppermute(block, "tm", route)


def to_owners(pieces):
    far = from_behind(pieces[2], 2)
    return [pieces[0], from_behind(pieces[1], 1), far, from_behind(pieces[3], 3)]


def sum_over_space(terms):
    for shift in (4, 2, 0):
        got = [terms] + [over_space(terms, m << shift) for m in (1, 2, 3)]
        if shift:
            terms = (got[0] + got[1]) + (got[2] + got[3])
    return got


def body(snapshots, tail, volume):
    snaps = jnp.transpose(snapshots, (1, 0, 2))
    tail = jnp.transpose(tail, (1, 0, 2))
    weights = volume.reshape(1, PDEV)
    band = jnp.asarray(banded_table())
    *first, edge = transform(band, snaps, ALL, 0, edge=True)
    early = to_owners(first)
    follow = lax.ppermute(edge, "tm", [(i, i - 1) for i in range(1, TM)])
    late = to_owners(transform(band, snaps, ALL, 1, (follow, tail)))
    terms, spec = gram_terms(ALL, ALL, early, late, weights)
    gram, modes = project(ALL, sum_over_space(terms), spec, ())
    return gram, jnp.transpose(modes, (0, 1, 3, 2, 4))


def solution(mesh):
    placed = (P("tm", None, "space"), P(None, None, "space"), P("space"))
    return jax.shard_map(
        body,
        mesh=mesh,
        in_specs=placed,
        out_specs=(P("tm", None, None, None), P("tm", None, None, None, "space")),
        check_vma=False,
    )
```

```python
import functools

import jax
import jax.numpy as jnp
import ml_dtypes
import numpy as np
from jax import lax
from jax.experimental import pallas as pl
from jax.experimental.pallas import tpu as pltpu
from jax.sharding import PartitionSpec as P

NB = 32
NFFT = 128
HOP = 64
SLOTS = 64
PDEV = 768
NPOINTS = 49152
TM = 4
OWN = NB // TM
HALF = OWN // 2
HERE = SLOTS // TM
BODY = HALF * HOP
ALL = (0, HERE // 2)
PARTS = ((0, 5), (5, HERE // 2))
LONG = 10**12
F32, BF16 = jnp.float32, jnp.bfloat16
ANY = pl.BlockSpec(memory_space=pl.ANY)
WHOLE, PART = 60 << 20, 16 << 20


def transform_table():
    f32 = np.float32
    times = np.arange(NFFT, dtype=f32)
    freq = np.arange(SLOTS, dtype=f32)[:, None]
    window = f32(0.5) - f32(0.5) * np.cos(f32(2.0 * np.pi) * times / f32(NFFT))
    window = window / np.sqrt(np.sum(window * window))
    angles = f32(2.0 * np.pi) * freq * times[None, :] / f32(NFFT)
    real_rows = window * np.cos(angles)
    imag_rows = -window * np.sin(angles)
    nyquist = window * np.cos(f32(np.pi) * times)
    imag_rows = np.where(freq == 0, nyquist[None, :], imag_rows)
    return np.stack([real_rows, imag_rows], axis=1).astype(ml_dtypes.bfloat16)


def banded_tables():
    table = transform_table()

    def band(starts, span):
        rows = np.zeros((SLOTS, 2, HALF, span), ml_dtypes.bfloat16)
        for b, start in enumerate(starts):
            rows[:, :, b, start : start + NFFT] = table
        return rows.reshape(TM, HERE * 2 * HALF, span)

    starts = [b * HOP for b in range(HALF)]
    late = [band(starts, BODY + 2 * HOP), band(starts[:-1] + [BODY], BODY + 2 * HOP)]
    return band(starts, BODY + HOP), np.concatenate(late, 0)


def core():
    return lax.axis_index("space") % 2


def pick(flag, yes, no):
    chosen = jnp.full(yes.shape, flag.astype(jnp.int32), jnp.int32) > 0
    return jnp.where(chosen, yes.astype(F32), no.astype(F32)).astype(BF16)


def apply_band(pairs, band, base, main, after, outs):
    rank = lax.axis_index("tm")
    first, stop = (4 * HALF * p for p in pairs)
    rows = jnp.concatenate([band[base + (rank + k) % TM, first:stop] for k in range(TM)], 0)
    got = jnp.dot(rows[:, :BODY], main, preferred_element_type=F32)
    got += jnp.dot(rows[:, BODY:], after, preferred_element_type=F32)
    got = got.astype(BF16).reshape(TM, pairs[1] - pairs[0], 4 * HALF, PDEV)
    for k, out in enumerate(outs):
        out[:, 0] = got[k]


def early_kernel(pairs, band, main, after, *outs):
    apply_band(pairs, band, 0, main[0], after[0], outs)


def late_kernel(pairs, band, main, head, moved, tail, *outs):
    rank = lax.axis_index("tm")
    half = pick((rank == TM - 1) & (core() == 0), tail[0], moved[0])
    start = pick((rank == 0) & (core() == 1), tail[0], head[0])
    apply_band(pairs, band, TM * core(), main[0], jnp.concatenate([half, start], 0), outs)


def transform(kernel, pairs, band, blocks, limit):
    count = pairs[1] - pairs[0]

    def block(span, at):
        return pl.BlockSpec((1, span, PDEV), lambda c: (c, at, 0))

    return pl.pallas_call(
        functools.partial(kernel, pairs),
        grid=(3,),
        in_specs=[pl.BlockSpec(band.shape, lambda c: (0, 0, 0))]
        + [block(span, at) for _, span, at in blocks],
        out_specs=[pl.BlockSpec((count, 1, 4 * HALF, PDEV), lambda c: (0, c, 0, 0))] * TM,
        out_shape=[jax.ShapeDtypeStruct((count, 3, 4 * HALF, PDEV), BF16)] * TM,
        compiler_params=pltpu.CompilerParams(vmem_limit_bytes=limit),
        cost_estimate=pl.CostEstimate(flops=LONG, bytes_accessed=0, transcendentals=0),
        name="transform",
    )(band, *(array for array, _, _ in blocks))


def zero_lanes(first_pair, pair):
    is_zero = (lax.axis_index("tm") == 0) & (pair + first_pair == 0)
    return jnp.where(is_zero, 2 * NB, 0)


def lane_masks():
    lane = lax.broadcasted_iota(jnp.int32, (NB, 4 * NB), 1)
    return lane, lane < 2 * NB, (lane % (2 * NB)) < NB


def gram_kernel(first_pair, *refs):
    early, late, volume = refs[:TM], refs[TM : 2 * TM], refs[2 * TM]
    terms, spec, held = refs[-3:]
    rank = lax.axis_index("tm")
    for k in range(TM):
        held[(rank + TM - k) % TM, 0] = early[k][0]
        held[(rank + TM - k) % TM, 1] = late[k][0]
    weights = volume[...]
    row = lax.broadcasted_iota(jnp.int32, (OWN, PDEV), 0)
    upper = row < HALF
    moved = (row % HALF) >= jnp.where(core() == 1, HALF - 1, HALF)
    total = jnp.zeros((4 * NB, 4 * NB), F32)
    for c in range(3):
        rows = []
        for s in range(2):
            real, imag = [], []
            for q in range(TM):
                a = held[q, 0, c].astype(F32)[s * OWN : (s + 1) * OWN]
                b = held[q, 1, c].astype(F32)[s * OWN : (s + 1) * OWN]
                after = held[(q + 1) % TM, 1, c].astype(F32)[s * OWN : (s + 1) * OWN]
                b = jnp.where(moved, after, b)
                real.append(jnp.where(upper, a, pltpu.roll(b, HALF, 0)))
                imag.append(jnp.where(upper, pltpu.roll(a, HALF, 0), b))
            rows += real + imag
        both = jnp.concatenate(rows, 0)
        plain = both.astype(BF16)
        weighted = (both * weights).astype(BF16)
        spec[0, c] = plain
        total += lax.dot_general(
            weighted, plain, (((1,), (1,)), ((), ())), preferred_element_type=F32
        )
    lane, first, low = lane_masks()
    top = jnp.where(first, total[:NB], total[2 * NB : 3 * NB])
    bottom = jnp.where(first, total[NB : 2 * NB], total[3 * NB :])
    summed = top + jnp.where(low, pltpu.roll(bottom, 3 * NB, 1), 0.0)
    apart = jnp.where(lane < NB, top, bottom)
    terms[0] = jnp.where(lane < zero_lanes(first_pair, pl.program_id(0)), apart, summed)


def gram_terms(group, pairs, early, late, volume, before=(), wait=(), cost=0):
    count = pairs[1] - pairs[0]
    skip = pairs[0] - group[0]
    size = group[1] - group[0]
    late_piece = pl.BlockSpec((1, 3, 4 * HALF, PDEV), lambda p: (p, 0, 0, 0))
    early_piece = pl.BlockSpec((1, 3, 4 * HALF, PDEV), lambda p: (p + skip, 0, 0, 0))
    return pl.pallas_call(
        functools.partial(gram_kernel, pairs[0]),
        grid=(count,),
        in_specs=[early_piece] * TM
        + [late_piece] * TM
        + [pl.BlockSpec((1, PDEV), lambda p: (0, 0))]
        + [ANY] * (len(before) + len(wait)),
        out_specs=[
            pl.BlockSpec((1, NB, 4 * NB), lambda p: (p + skip, 0, 0)),
            pl.BlockSpec((1, 3, 4 * NB, PDEV), lambda p: (p + skip, 0, 0, 0)),
        ],
        out_shape=[
            jax.ShapeDtypeStruct((size, NB, 4 * NB), F32),
            jax.ShapeDtypeStruct((size, 3, 4 * NB, PDEV), BF16),
        ],
        scratch_shapes=[pltpu.VMEM((TM, 2, 3, 4 * HALF, PDEV), BF16)],
        input_output_aliases={2 * TM + 1 + i: i for i in range(len(before))},
        compiler_params=pltpu.CompilerParams(vmem_limit_bytes=PART),
        cost_estimate=pl.CostEstimate(flops=cost, bytes_accessed=0, transcendentals=0),
        name="gram_terms",
    )(*early, *late, volume, *before, *wait)


def mix(first_pair, pair, total):
    lane, first, low = lane_masks()
    zero = lane < zero_lanes(first_pair, pair)
    flipped = jnp.concatenate([total] * 4, 0).T
    cross_t = jnp.where(first, flipped[NB : 2 * NB], flipped[3 * NB :])
    mat = jnp.where(low, total, jnp.where(zero, total, total - cross_t))
    squares = mat * mat

    def part_sum(keep):
        return jnp.sum(jnp.where(keep, squares, 0.0), keepdims=True)

    e0, e1 = part_sum(lane < NB), part_sum(first & ~low)
    rest_sum = part_sum(~first)
    zero_here = zero[:1, :1]
    norm_a = jnp.sqrt(jnp.where(zero_here, e0, e0 + e1) + 1e-06)
    norm_b = jnp.sqrt(jnp.where(zero_here, e1, e0 + e1) + 1e-06)
    norm_rest = jnp.sqrt(rest_sum + 1e-06)
    turned = jnp.where(low, -pltpu.roll(mat, 3 * NB, 1), pltpu.roll(mat, NB, 1))
    part_a = jnp.where(zero, jnp.where(low, mat, 0.0), mat)
    part_b = jnp.where(zero, jnp.where(low, 0.0, mat), turned)
    part_a = part_a / jnp.where(first, norm_a, norm_rest)
    part_b = part_b / jnp.where(first, norm_b, norm_rest)
    mixing = jnp.concatenate(
        [
            jnp.where(first, part_a, 0.0),
            jnp.where(first, part_b, 0.0),
            jnp.where(first, 0.0, part_a),
            jnp.where(first, 0.0, part_b),
        ],
        0,
    )
    return mat, mixing.astype(BF16)


def modes_kernel(pairs, t0, t1, t2, t3, spec, *rest):
    gram, modes, mats, mixings = rest[-4:]
    pair = pl.program_id(0)

    @pl.when(pair == 0)
    def _():
        for p in range(pairs[1] - pairs[0]):
            total = ((t0[p] + t1[p]) + (t2[p] + t3[p])) / (NB * 3 * NPOINTS)
            mats[p], mixings[p] = mix(pairs[0], p, total)

    mat = mats[pair]
    for s in range(2):
        for part in range(2):
            at = (2 * s + part) * NB
            gram[s, part] = mat[:, at : at + NB]
    for c in range(3):
        got = jnp.dot(mixings[pair], spec[0, c], preferred_element_type=F32)
        modes[:, :, c] = got.astype(BF16).reshape(2, 2, NB, PDEV)


def project(pairs, totals, spec, before):
    first, count = pairs[0], pairs[1] - pairs[0]
    return pl.pallas_call(
        functools.partial(modes_kernel, pairs),
        grid=(count,),
        in_specs=[pl.BlockSpec((count, NB, 4 * NB), lambda p: (0, 0, 0))] * 4
        + [pl.BlockSpec((1, 3, 4 * NB, PDEV), lambda p: (p, 0, 0, 0))]
        + [ANY] * len(before),
        out_specs=[
            pl.BlockSpec((2, 2, NB, NB), lambda p: (p + first, 0, 0, 0)),
            pl.BlockSpec((2, 2, 3, NB, PDEV), lambda p: (p + first, 0, 0, 0, 0)),
        ],
        out_shape=[
            jax.ShapeDtypeStruct((HERE, 2, NB, NB), F32),
            jax.ShapeDtypeStruct((HERE, 2, 3, NB, PDEV), BF16),
        ],
        scratch_shapes=[
            pltpu.VMEM((count, NB, 4 * NB), F32),
            pltpu.VMEM((count, 4 * NB, 4 * NB), BF16),
        ],
        input_output_aliases={5 + i: i for i in range(len(before))},
        compiler_params=pltpu.CompilerParams(vmem_limit_bytes=PART),
        cost_estimate=pl.CostEstimate(flops=0, bytes_accessed=0, transcendentals=0),
        name="modes",
    )(*totals, spec, *before)


def over_space(block, mask):
    route = [(i, i ^ mask) for i in range(lax.axis_size("space"))]
    return lax.ppermute(block, "space", route)


def half_block_route():
    route = []
    for s in range(lax.axis_size("space")):
        for t in range(TM):
            if s % 2 == 1:
                route.append((s * TM + t, s * TM + (t + 1) % TM))
            elif t:
                route.append((s * TM + t, s * TM + t - 1))
    return route


def from_behind(block, distance):
    route = [(i, (i + distance) % TM) for i in range(TM)]
    return lax.ppermute(block, "tm", route)


def to_owners(pieces):
    far = from_behind(pieces[2], 2)
    return [pieces[0], from_behind(pieces[1], 1), far, from_behind(pieces[3], 3)]


def sum_over_space(terms):
    for shift in (4, 2, 0):
        got = [terms] + [over_space(terms, m << shift) for m in (1, 2, 3)]
        if shift:
            terms = (got[0] + got[1]) + (got[2] + got[3])
    return got


def body(snapshots, tail, volume):
    snaps = jnp.transpose(snapshots, (1, 0, 2))
    tail = jnp.transpose(tail, (1, 0, 2))
    weights = volume.reshape(1, PDEV)
    early_band, late_band = (jnp.asarray(b) for b in banded_tables())
    edge = lax.dynamic_slice_in_dim(snaps, core() * (OWN - 1) * HOP, HOP, 1)
    moved = lax.ppermute(edge, ("space", "tm"), half_block_route())
    blocks = [(snaps, BODY, 0), (snaps, HOP, HALF)]
    early = to_owners(transform(early_kernel, ALL, early_band, blocks, WHOLE))
    blocks = [(snaps, BODY, 1), (snaps, HOP, 0), (moved, HOP, 0), (tail, HOP, 0)]
    late = [transform(late_kernel, part, late_band, blocks, PART) for part in PARTS]
    late = [to_owners(pieces) for pieces in late]
    sums = gram_terms(ALL, PARTS[0], early, late[0], weights, cost=LONG)
    terms, spec = gram_terms(ALL, PARTS[1], early, late[1], weights, sums)
    gram, modes = project(ALL, sum_over_space(terms), spec, ())
    return gram, jnp.transpose(modes, (0, 1, 3, 2, 4))


def solution(mesh):
    placed = (P("tm", None, "space"), P(None, None, "space"), P("space"))
    return jax.shard_map(
        body,
        mesh=mesh,
        in_specs=placed,
        out_specs=(P("tm", None, None, None), P("tm", None, None, None, "space")),
        check_vma=False,
    )
```

```python
import functools

import jax
import jax.numpy as jnp
import ml_dtypes
import numpy as np
from jax import lax
from jax.experimental import pallas as pl
from jax.experimental.pallas import tpu as pltpu
from jax.sharding import PartitionSpec as P

NB = 32
NFFT = 128
HOP = 64
SLOTS = 64
PDEV = 768
NPOINTS = 49152
TM = 4
OWN = NB // TM
HALF = OWN // 2
HERE = SLOTS // TM
BODY = HALF * HOP
ALL = (0, HERE // 2)
QUADS = HERE // 4
PARTS = ((0, 3), (3, QUADS))
LONG = 10**12
F32, BF16 = jnp.float32, jnp.bfloat16
ANY = pl.BlockSpec(memory_space=pl.ANY)
WHOLE, PART = 60 << 20, 16 << 20


def transform_table():
    f32 = np.float32
    times = np.arange(NFFT, dtype=f32)
    freq = np.arange(SLOTS, dtype=f32)[:, None]
    window = f32(0.5) - f32(0.5) * np.cos(f32(2.0 * np.pi) * times / f32(NFFT))
    window = window / np.sqrt(np.sum(window * window))
    angles = f32(2.0 * np.pi) * freq * times[None, :] / f32(NFFT)
    real_rows = window * np.cos(angles)
    imag_rows = -window * np.sin(angles)
    nyquist = window * np.cos(f32(np.pi) * times)
    imag_rows = np.where(freq == 0, nyquist[None, :], imag_rows)
    return np.stack([real_rows, imag_rows], axis=1).astype(ml_dtypes.bfloat16)


def banded_tables():
    table = transform_table()

    def band(starts, span):
        rows = np.zeros((SLOTS, 2, HALF, span), ml_dtypes.bfloat16)
        for b, start in enumerate(starts):
            rows[:, :, b, start : start + NFFT] = table
        return rows.reshape(TM, HERE * 2 * HALF, span)

    starts = [b * HOP for b in range(HALF)]
    late = [band(starts, BODY + 2 * HOP), band(starts[:-1] + [BODY], BODY + 2 * HOP)]
    return band(starts, BODY + HOP), np.concatenate(late, 0)


def core():
    return lax.axis_index("space") % 2


def pick(flag, yes, no):
    chosen = jnp.full(yes.shape, flag.astype(jnp.int32), jnp.int32) > 0
    return jnp.where(chosen, yes.astype(F32), no.astype(F32)).astype(BF16)


def apply_band(pairs, band, base, main, after, outs):
    rank = lax.axis_index("tm")
    first, stop = (4 * HALF * p for p in pairs)
    rows = jnp.concatenate([band[base + (rank + k) % TM, first:stop] for k in range(TM)], 0)
    got = jnp.dot(rows[:, :BODY], main, preferred_element_type=F32)
    got += jnp.dot(rows[:, BODY:], after, preferred_element_type=F32)
    got = got.astype(BF16).reshape(TM, pairs[1] - pairs[0], 4 * HALF, PDEV)
    for k, out in enumerate(outs):
        out[:, 0] = got[k]


def early_kernel(pairs, band, main, after, *outs):
    apply_band(pairs, band, 0, main[0], after[0], outs)


def late_kernel(pairs, band, main, head, moved, tail, *outs):
    rank = lax.axis_index("tm")
    half = pick((rank == TM - 1) & (core() == 0), tail[0], moved[0])
    start = pick((rank == 0) & (core() == 1), tail[0], head[0])
    apply_band(pairs, band, TM * core(), main[0], jnp.concatenate([half, start], 0), outs)


def transform(kernel, pairs, band, blocks, limit):
    count = pairs[1] - pairs[0]

    def block(span, at):
        return pl.BlockSpec((1, span, PDEV), lambda c: (c, at, 0))

    return pl.pallas_call(
        functools.partial(kernel, pairs),
        grid=(3,),
        in_specs=[pl.BlockSpec(band.shape, lambda c: (0, 0, 0))]
        + [block(span, at) for _, span, at in blocks],
        out_specs=[pl.BlockSpec((count, 1, 4 * HALF, PDEV), lambda c: (0, c, 0, 0))] * TM,
        out_shape=[jax.ShapeDtypeStruct((count, 3, 4 * HALF, PDEV), BF16)] * TM,
        compiler_params=pltpu.CompilerParams(vmem_limit_bytes=limit),
        cost_estimate=pl.CostEstimate(flops=LONG, bytes_accessed=0, transcendentals=0),
        name="transform",
    )(band, *(array for array, _, _ in blocks))


def zero_lanes(is_first, lanes):
    return jnp.where((lax.axis_index("tm") == 0) & is_first, lanes, 0)


def lane_masks():
    lane = lax.broadcasted_iota(jnp.int32, (NB, 4 * NB), 1)
    return lane, lane < 2 * NB, (lane % (2 * NB)) < NB


def triangle():
    row = lax.broadcasted_iota(jnp.int32, (NB, 4 * NB), 0)
    return row, lax.broadcasted_iota(jnp.int32, (NB, 4 * NB), 1) % NB


def by_quarter(parts):
    lane, _, _ = lane_masks()
    out = parts[3]
    for at in (2, 1, 0):
        out = jnp.where(lane < (at + 1) * NB, parts[at], out)
    return out


def turn(x, quarters):
    return pltpu.roll(x, (quarters % 4) * NB, 1) if quarters % 4 else x


def transposed(four):
    flipped = jnp.concatenate([four] * 4, 0).T
    return by_quarter([flipped[g * NB : (g + 1) * NB] for g in range(4)])


def pair_terms(early, late, volume, spec, pair, is_first):
    rank = lax.axis_index("tm")
    row = lax.broadcasted_iota(jnp.int32, (OWN, PDEV), 0)
    upper = row < HALF
    moved = (row % HALF) >= jnp.where(core() == 1, HALF - 1, HALF)
    weights = volume[...]
    total = jnp.zeros((4 * NB, 4 * NB), F32)
    for c in range(3):
        rows = []
        for s in range(2):
            half = slice(s * OWN, (s + 1) * OWN)
            real, imag = [], []
            for q in range(TM):
                a = early[q, pair, c].astype(F32)[half]
                b = late[q, pair, c].astype(F32)[half]
                after = late[(q + 1) % TM, pair, c].astype(F32)[half]
                b = jnp.where(moved, after, b)
                real.append(jnp.where(upper, a, pltpu.roll(b, HALF, 0)))
                imag.append(jnp.where(upper, pltpu.roll(a, HALF, 0), b))
            rows += real + imag
        both = jnp.concatenate(rows, 0)
        plain = both.astype(BF16)
        weighted = (both * weights).astype(BF16)
        spec[pair, c] = plain
        total += lax.dot_general(
            weighted, plain, (((1,), (1,)), ((), ())), preferred_element_type=F32
        )
    lane, first, low = lane_masks()
    top = jnp.where(first, total[:NB], total[2 * NB : 3 * NB])
    bottom = jnp.where(first, total[NB : 2 * NB], total[3 * NB :])
    summed = top + jnp.where(low, turn(bottom, 3), 0.0)
    if pair:
        return summed
    apart = jnp.where(lane < NB, top, bottom)
    return jnp.where(lane < zero_lanes(is_first, 2 * NB), apart, summed)


def gram_kernel(quads, *refs):
    pieces, volume = refs[: 2 * TM], refs[2 * TM]
    terms, spec, early, late = refs[-4:]
    step = pl.program_id(0)
    rank = lax.axis_index("tm")
    for k in range(TM):
        early[(rank + TM - k) % TM] = pieces[k][...]
        late[(rank + TM - k) % TM] = pieces[TM + k][...]

    is_first = step + quads[0] == 0
    if quads[0]:

        @pl.when(step == 0)
        def _():
            terms[...] = refs[2 * TM + 1][...]

    one, two = (pair_terms(early, late, volume, spec, p, is_first) for p in range(2))
    sums = by_quarter([one, turn(one, -1), turn(two, 2), turn(two, 1)])
    cross = by_quarter([turn(one, -1), turn(one, -2), turn(two, 1), two])
    lane, _, _ = lane_masks()
    zero = lane < zero_lanes(is_first, NB)
    row, column = triangle()
    below = jnp.where(zero, cross, cross - transposed(cross))
    at = pl.multiple_of((step + quads[0]) * NB, NB)
    terms[pl.ds(at, NB)] = jnp.where(row <= column, sums, below)
    if not quads[0]:

        @pl.when(step == 0)
        def _():
            diagonal = jnp.sum(jnp.where(row == column, cross, 0.0), 0, keepdims=True)
            terms[QUADS * NB :] = jnp.broadcast_to(diagonal, (8, 4 * NB))


def gram_terms(quads, early, late, volume, before=(), cost=0):
    count, skip = quads[1] - quads[0], quads[0]
    block = (2, 3, 4 * HALF, PDEV)
    whole = ((QUADS * NB + 8), 4 * NB)
    return pl.pallas_call(
        functools.partial(gram_kernel, quads),
        grid=(count,),
        in_specs=[pl.BlockSpec(block, lambda p: (p + skip, 0, 0, 0))] * TM
        + [pl.BlockSpec(block, lambda p: (p, 0, 0, 0))] * TM
        + [pl.BlockSpec((1, PDEV), lambda p: (0, 0))]
        + [pl.BlockSpec(whole, lambda p: (0, 0)), ANY][: len(before)],
        out_specs=[
            pl.BlockSpec(whole, lambda p: (0, 0)),
            pl.BlockSpec((2, 3, 4 * NB, PDEV), lambda p: (p + skip, 0, 0, 0)),
        ],
        out_shape=[
            jax.ShapeDtypeStruct(whole, F32),
            jax.ShapeDtypeStruct((2 * QUADS, 3, 4 * NB, PDEV), BF16),
        ],
        scratch_shapes=[pltpu.VMEM((TM,) + block, BF16)] * 2,
        input_output_aliases={2 * TM + 2: 1} if before else {},
        compiler_params=pltpu.CompilerParams(vmem_limit_bytes=PART),
        cost_estimate=pl.CostEstimate(flops=cost, bytes_accessed=0, transcendentals=0),
        name="gram_terms",
    )(*early, *late, volume, *before)


def mix(mat, is_first):
    lane, first, low = lane_masks()
    zero = lane < zero_lanes(is_first, 2 * NB)
    squares = mat * mat

    def part_sum(keep):
        return jnp.sum(jnp.where(keep, squares, 0.0), keepdims=True)

    e0, e1 = part_sum(lane < NB), part_sum(first & ~low)
    rest_sum = part_sum(~first)
    zero_here = zero[:1, :1]
    norm_a = jnp.sqrt(jnp.where(zero_here, e0, e0 + e1) + 1e-06)
    norm_b = jnp.sqrt(jnp.where(zero_here, e1, e0 + e1) + 1e-06)
    norm_rest = jnp.sqrt(rest_sum + 1e-06)
    turned = jnp.where(low, -turn(mat, 3), turn(mat, 1))
    part_a = jnp.where(zero, jnp.where(low, mat, 0.0), mat)
    part_b = jnp.where(zero, jnp.where(low, 0.0, mat), turned)
    part_a = part_a / jnp.where(first, norm_a, norm_rest)
    part_b = part_b / jnp.where(first, norm_b, norm_rest)
    mixing = jnp.concatenate(
        [
            jnp.where(first, part_a, 0.0),
            jnp.where(first, part_b, 0.0),
            jnp.where(first, 0.0, part_a),
            jnp.where(first, 0.0, part_b),
        ],
        0,
    )
    return mixing.astype(BF16)


def modes_kernel(t0, t1, t2, t3, spec, gram, modes, mats, mixings):
    pair = pl.program_id(0)

    @pl.when(pair == 0)
    def _():
        total = ((t0[...] + t1[...]) + (t2[...] + t3[...])) / (NB * 3 * NPOINTS)
        row, column = triangle()
        lane, _, _ = lane_masks()
        for u in range(QUADS):
            packed = total[u * NB : (u + 1) * NB]
            other = transposed(packed)
            even = jnp.where(row <= column, packed, other)
            odd = jnp.where(row > column, packed, jnp.where(row < column, -other, 0.0))
            if u == 0:
                diagonal = total[QUADS * NB : QUADS * NB + 1]
                alone = jnp.where(row < column, other, jnp.where(row > column, packed, diagonal))
                odd = jnp.where(lane < zero_lanes(True, NB), alone, odd)
            one = by_quarter([even, turn(odd, 1), turn(even, 1), turn(odd, 2)])
            two = by_quarter([turn(even, 2), turn(odd, -1), turn(even, -1), odd])
            mats[2 * u], mats[2 * u + 1] = one, two
            mixings[2 * u], mixings[2 * u + 1] = mix(one, u == 0), mix(two, False)

    mat = mats[pair]
    for s in range(2):
        for part in range(2):
            at = (2 * s + part) * NB
            gram[s, part] = mat[:, at : at + NB]
    for c in range(3):
        got = jnp.dot(mixings[pair], spec[0, c], preferred_element_type=F32)
        modes[:, :, c] = got.astype(BF16).reshape(2, 2, NB, PDEV)


def project(totals, spec):
    return pl.pallas_call(
        modes_kernel,
        grid=(2 * QUADS,),
        in_specs=[pl.BlockSpec(totals[0].shape, lambda p: (0, 0))] * 4
        + [pl.BlockSpec((1, 3, 4 * NB, PDEV), lambda p: (p, 0, 0, 0))],
        out_specs=[
            pl.BlockSpec((2, 2, NB, NB), lambda p: (p, 0, 0, 0)),
            pl.BlockSpec((2, 2, 3, NB, PDEV), lambda p: (p, 0, 0, 0, 0)),
        ],
        out_shape=[
            jax.ShapeDtypeStruct((HERE, 2, NB, NB), F32),
            jax.ShapeDtypeStruct((HERE, 2, 3, NB, PDEV), BF16),
        ],
        scratch_shapes=[
            pltpu.VMEM((2 * QUADS, NB, 4 * NB), F32),
            pltpu.VMEM((2 * QUADS, 4 * NB, 4 * NB), BF16),
        ],
        compiler_params=pltpu.CompilerParams(vmem_limit_bytes=PART),
        cost_estimate=pl.CostEstimate(flops=0, bytes_accessed=0, transcendentals=0),
        name="modes",
    )(*totals, spec)


def over_space(block, mask):
    route = [(i, i ^ mask) for i in range(lax.axis_size("space"))]
    return lax.ppermute(block, "space", route)


def half_block_route():
    route = []
    for s in range(lax.axis_size("space")):
        for t in range(TM):
            if s % 2 == 1:
                route.append((s * TM + t, s * TM + (t + 1) % TM))
            elif t:
                route.append((s * TM + t, s * TM + t - 1))
    return route


def from_behind(block, distance):
    route = [(i, (i + distance) % TM) for i in range(TM)]
    return lax.ppermute(block, "tm", route)


def to_owners(pieces):
    far = from_behind(pieces[2], 2)
    return [pieces[0], from_behind(pieces[1], 1), far, from_behind(pieces[3], 3)]


def sum_over_space(terms):
    for shift in (4, 2, 0):
        got = [terms] + [over_space(terms, m << shift) for m in (1, 2, 3)]
        if shift:
            terms = (got[0] + got[1]) + (got[2] + got[3])
    return got


def body(snapshots, tail, volume):
    snaps = jnp.transpose(snapshots, (1, 0, 2))
    tail = jnp.transpose(tail, (1, 0, 2))
    weights = volume.reshape(1, PDEV)
    early_band, late_band = (jnp.asarray(b) for b in banded_tables())
    edge = lax.dynamic_slice_in_dim(snaps, core() * (OWN - 1) * HOP, HOP, 1)
    moved = lax.ppermute(edge, ("space", "tm"), half_block_route())
    blocks = [(snaps, BODY, 0), (snaps, HOP, HALF)]
    early = to_owners(transform(early_kernel, ALL, early_band, blocks, WHOLE))
    blocks = [(snaps, BODY, 1), (snaps, HOP, 0), (moved, HOP, 0), (tail, HOP, 0)]
    late = [transform(late_kernel, (2 * a, 2 * b), late_band, blocks, PART) for a, b in PARTS]
    late = [to_owners(pieces) for pieces in late]
    sums = gram_terms(PARTS[0], early, late[0], weights, cost=LONG)
    terms, spec = gram_terms(PARTS[1], early, late[1], weights, sums)
    gram, modes = project(sum_over_space(terms), spec)
    return gram, jnp.transpose(modes, (0, 1, 3, 2, 4))


def solution(mesh):
    placed = (P("tm", None, "space"), P(None, None, "space"), P("space"))
    return jax.shard_map(
        body,
        mesh=mesh,
        in_specs=placed,
        out_specs=(P("tm", None, None, None), P("tm", None, None, None, "space")),
        check_vma=False,
    )
```

```python
import functools

import jax
import jax.numpy as jnp
import ml_dtypes
import numpy as np
from jax import lax
from jax.experimental import pallas as pl
from jax.experimental.pallas import tpu as pltpu
from jax.sharding import PartitionSpec as P

NB = 32
NFFT = 128
HOP = 64
SLOTS = 64
PDEV = 768
NPOINTS = 49152
TM = 4
OWN = NB // TM
HALF = OWN // 2
HERE = SLOTS // TM
BODY = HALF * HOP
ALL = (0, HERE // 2)
PAIRS, QUADS = HERE // 2, HERE // 4
LANES = 256
LONG = 10**12
F32, BF16 = jnp.float32, jnp.bfloat16
HELD = pl.BlockSpec(memory_space=pltpu.VMEM)
WHOLE, PART = 60 << 20, 16 << 20


def transform_table():
    f32 = np.float32
    times = np.arange(NFFT, dtype=f32)
    freq = np.arange(SLOTS, dtype=f32)[:, None]
    window = f32(0.5) - f32(0.5) * np.cos(f32(2.0 * np.pi) * times / f32(NFFT))
    window = window / np.sqrt(np.sum(window * window))
    angles = f32(2.0 * np.pi) * freq * times[None, :] / f32(NFFT)
    real_rows = window * np.cos(angles)
    imag_rows = -window * np.sin(angles)
    nyquist = window * np.cos(f32(np.pi) * times)
    imag_rows = np.where(freq == 0, nyquist[None, :], imag_rows)
    return np.stack([real_rows, imag_rows], axis=1).astype(ml_dtypes.bfloat16)


def banded_tables():
    table = transform_table()

    def band(starts, span):
        rows = np.zeros((SLOTS, 2, HALF, span), ml_dtypes.bfloat16)
        for b, start in enumerate(starts):
            rows[:, :, b, start : start + NFFT] = table
        return rows.reshape(TM, HERE * 2 * HALF, span)

    starts = [b * HOP for b in range(HALF)]
    late = [band(starts, BODY + 2 * HOP), band(starts[:-1] + [BODY], BODY + 2 * HOP)]
    return band(starts, BODY + HOP), np.concatenate(late, 0)


def orders():
    arrived = np.arange(4 * NB)
    piece, s, ri, b = arrived // 16, arrived // 8 % 2, arrived // 4 % 2, arrived % 4
    late, distance = piece // TM, piece % TM
    out = np.zeros((2 * TM, 4 * NB, 4 * NB), ml_dtypes.bfloat16)
    for rank in range(TM):
        for which in range(2):
            moved = which * late * (b == HALF - 1)
            source = (rank - distance - moved) % TM
            natural = s * 64 + ri * NB + source * OWN + late * HALF + b
            out[2 * rank + which, natural, arrived] = 1
    return out


def core():
    return lax.axis_index("space") % 2


def pick(flag, yes, no):
    chosen = jnp.full(yes.shape, flag.astype(jnp.int32), jnp.int32) > 0
    return jnp.where(chosen, yes.astype(F32), no.astype(F32)).astype(BF16)


def apply_band(pairs, band, base, main, after, outs):
    rank = lax.axis_index("tm")
    first, stop = (4 * HALF * p for p in pairs)
    rows = jnp.concatenate([band[base + (rank + k) % TM, first:stop] for k in range(TM)], 0)
    got = jnp.dot(rows[:, :BODY], main, preferred_element_type=F32)
    got += jnp.dot(rows[:, BODY:], after, preferred_element_type=F32)
    got = got.astype(BF16).reshape(TM, pairs[1] - pairs[0], 4 * HALF, PDEV)
    for k, out in enumerate(outs):
        out[:, pl.program_id(0)] = got[k]


def early_kernel(pairs, band, main, after, *outs):
    apply_band(pairs, band, 0, main[0], after[0], outs)


def late_kernel(pairs, band, main, head, moved, tail, *outs):
    rank = lax.axis_index("tm")
    half = pick((rank == TM - 1) & (core() == 0), tail[0], moved[0])
    start = pick((rank == 0) & (core() == 1), tail[0], head[0])
    apply_band(pairs, band, TM * core(), main[0], jnp.concatenate([half, start], 0), outs)


def transform(kernel, pairs, band, blocks, limit):
    count = pairs[1] - pairs[0]

    def block(span, at):
        return pl.BlockSpec((1, span, PDEV), lambda c: (c, at, 0))

    return pl.pallas_call(
        functools.partial(kernel, pairs),
        grid=(3,),
        in_specs=[pl.BlockSpec(band.shape, lambda c: (0, 0, 0))]
        + [block(span, at) for _, span, at in blocks],
        out_specs=[HELD] * TM,
        out_shape=[jax.ShapeDtypeStruct((count, 3, 4 * HALF, PDEV), BF16)] * TM,
        compiler_params=pltpu.CompilerParams(vmem_limit_bytes=limit),
        cost_estimate=pl.CostEstimate(flops=LONG, bytes_accessed=0, transcendentals=0),
        name="transform",
    )(band, *(array for array, _, _ in blocks))


def zero_lanes(is_first, lanes):
    return jnp.where((lax.axis_index("tm") == 0) & is_first, lanes, 0)


def lane_masks():
    lane = lax.broadcasted_iota(jnp.int32, (NB, 4 * NB), 1)
    return lane, lane < 2 * NB, (lane % (2 * NB)) < NB


def triangle():
    row = lax.broadcasted_iota(jnp.int32, (NB, 4 * NB), 0)
    return row, lax.broadcasted_iota(jnp.int32, (NB, 4 * NB), 1) % NB


def by_quarter(parts):
    lane, _, _ = lane_masks()
    out = parts[3]
    for at in (2, 1, 0):
        out = jnp.where(lane < (at + 1) * NB, parts[at], out)
    return out


def turn(x, quarters):
    return pltpu.roll(x, (quarters % 4) * NB, 1) if quarters % 4 else x


def transposed(four):
    flipped = jnp.concatenate([four] * 4, 0).T
    return by_quarter([flipped[g * NB : (g + 1) * NB] for g in range(4)])


def rows_of(pieces, pair, c, lanes=slice(None)):
    return [p[pair, c, :, lanes] for p in pieces]


def in_three(x):
    high = x.astype(BF16)
    rest = x - high.astype(F32)
    middle = rest.astype(BF16)
    return [high, middle, (rest - middle.astype(F32)).astype(BF16)]


def reorder(x, order):
    n = x.shape[0]
    got = lax.dot_general(
        jnp.concatenate(in_three(x), 0),
        order,
        (((1,), (1,)), ((), ())),
        preferred_element_type=F32,
    )
    x = (got[:n] + got[n : 2 * n]) + got[2 * n :]
    x = jnp.concatenate([x[at : at + 4 * NB] for at in range(0, n, 4 * NB)], 1)
    got = jnp.dot(order, jnp.concatenate(in_three(x), 1), preferred_element_type=F32)
    return (got[:, :n] + got[:, n : 2 * n]) + got[:, 2 * n :]


def pair_terms(total, is_zero):
    lane, first, low = lane_masks()
    top = jnp.where(first, total[:NB], total[2 * NB : 3 * NB])
    bottom = jnp.where(first, total[NB : 2 * NB], total[3 * NB :])
    summed = top + jnp.where(low, turn(bottom, 3), 0.0)
    if not is_zero:
        return summed
    apart = jnp.where(lane < NB, top, bottom)
    return jnp.where(lane < zero_lanes(True, 2 * NB), apart, summed)


def gram_kernel(*refs):
    pieces, (volume, orders, terms, sums) = refs[: 2 * TM], refs[2 * TM :]
    quad, n = pl.program_id(0), 4 * NB
    total = jnp.zeros((2 * n, 2 * n), F32)
    for c in range(3):
        for start in range(0, PDEV, LANES):
            lanes = slice(start, start + LANES)
            weights = volume[:, lanes]
            rows = rows_of(pieces, 2 * quad, c, lanes) + rows_of(pieces, 2 * quad + 1, c, lanes)
            weighted = [(r.astype(F32) * weights).astype(BF16) for r in rows]
            total += lax.dot_general(
                jnp.concatenate(weighted, 0),
                jnp.concatenate(rows, 0),
                (((1,), (1,)), ((), ())),
                preferred_element_type=F32,
            )
    sums[2 * quad] = total[:n, :n]
    sums[2 * quad + 1] = total[n:, n:]

    @pl.when(quad == QUADS - 1)
    def _():
        order = orders[2 * lax.axis_index("tm") + core()]
        every = reorder(sums[...].reshape(PAIRS * n, n), order)
        lane, _, _ = lane_masks()
        row, column = triangle()
        for u in range(QUADS):
            one, two = (
                pair_terms(every[:, p * n : (p + 1) * n], p == 0) for p in (2 * u, 2 * u + 1)
            )
            plus = by_quarter([one, turn(one, -1), turn(two, 2), turn(two, 1)])
            cross = by_quarter([turn(one, -1), turn(one, -2), turn(two, 1), two])
            below = cross - transposed(cross)
            if u == 0:
                below = jnp.where(lane < zero_lanes(True, NB), cross, below)
                diagonal = jnp.sum(jnp.where(row == column, cross, 0.0), 0, keepdims=True)
                terms[QUADS * NB :] = jnp.broadcast_to(diagonal, (8, 4 * NB))
            terms[u * NB : (u + 1) * NB] = jnp.where(row <= column, plus, below)


def gram_terms(pieces, volume, order):
    return pl.pallas_call(
        gram_kernel,
        grid=(QUADS,),
        in_specs=[HELD] * (2 * TM + 2),
        out_specs=HELD,
        out_shape=jax.ShapeDtypeStruct((QUADS * NB + 8, 4 * NB), F32),
        scratch_shapes=[pltpu.VMEM((PAIRS, 4 * NB, 4 * NB), F32)],
        compiler_params=pltpu.CompilerParams(vmem_limit_bytes=PART),
        cost_estimate=pl.CostEstimate(flops=0, bytes_accessed=0, transcendentals=0),
        name="gram_terms",
    )(*pieces, volume, order)


def mix(mat, is_first):
    lane, first, low = lane_masks()
    zero = lane < (zero_lanes(True, 2 * NB) if is_first else 0)
    squares = mat * mat

    def part_sum(keep):
        return jnp.sum(jnp.where(keep, squares, 0.0), keepdims=True)

    e0, e1 = part_sum(lane < NB), part_sum(first & ~low)
    rest_sum = part_sum(~first)
    zero_here = zero[:1, :1]
    norm_a = jnp.sqrt(jnp.where(zero_here, e0, e0 + e1) + 1e-06)
    norm_b = jnp.sqrt(jnp.where(zero_here, e1, e0 + e1) + 1e-06)
    norm_rest = jnp.sqrt(rest_sum + 1e-06)
    turned = jnp.where(low, -turn(mat, 3), turn(mat, 1))
    part_a = jnp.where(zero, jnp.where(low, mat, 0.0), mat)
    part_b = jnp.where(zero, jnp.where(low, 0.0, mat), turned)
    part_a = part_a / jnp.where(first, norm_a, norm_rest)
    part_b = part_b / jnp.where(first, norm_b, norm_rest)
    mixing = jnp.concatenate(
        [
            jnp.where(first, part_a, 0.0),
            jnp.where(first, part_b, 0.0),
            jnp.where(first, 0.0, part_a),
            jnp.where(first, 0.0, part_b),
        ],
        0,
    )
    return mixing.astype(BF16)


def modes_kernel(t0, t1, t2, t3, orders, *refs):
    pieces = refs[: 2 * TM]
    gram_out, modes_out, gram, modes, sems = refs[2 * TM :]
    order = orders[2 * lax.axis_index("tm") + core()]
    total = ((t0[...] + t1[...]) + (t2[...] + t3[...])) / (NB * 3 * NPOINTS)
    row, column = triangle()
    lane, _, _ = lane_masks()
    copies = []
    for u in range(QUADS):
        packed = total[u * NB : (u + 1) * NB]
        other = transposed(packed)
        even = jnp.where(row <= column, packed, other)
        odd = jnp.where(row > column, packed, jnp.where(row < column, -other, 0.0))
        if u == 0:
            diagonal = total[QUADS * NB : QUADS * NB + 1]
            alone = jnp.where(row < column, other, jnp.where(row > column, packed, diagonal))
            odd = jnp.where(lane < zero_lanes(True, NB), alone, odd)
        one = by_quarter([even, turn(odd, 1), turn(even, 1), turn(odd, 2)])
        two = by_quarter([turn(even, 2), turn(odd, -1), turn(even, -1), odd])
        for pair, mat in ((2 * u, one), (2 * u + 1, two)):
            for s in range(2):
                for part in range(2):
                    at = (2 * s + part) * NB
                    gram[2 * pair + s, part] = mat[:, at : at + NB]
            mixing = mix(mat, True if pair == 0 else False)
            mixing = jnp.dot(mixing, order, preferred_element_type=F32).astype(BF16)
            slots = pl.ds(2 * pair, 2)
            for c in range(3):
                rows = jnp.concatenate(rows_of(pieces, pair, c), 0)
                got = jnp.dot(mixing, rows, preferred_element_type=F32)
                modes[slots, :, c] = got.astype(BF16).reshape(2, 2, NB, PDEV)
            copies.append(pltpu.make_async_copy(modes.at[slots], modes_out.at[slots], sems.at[pair]))
            copies[-1].start()
    copies.append(pltpu.make_async_copy(gram, gram_out, sems.at[PAIRS]))
    copies[-1].start()
    for copy in copies:
        copy.wait()


def project(totals, order, pieces):
    gram = jax.ShapeDtypeStruct((HERE, 2, NB, NB), F32)
    modes = jax.ShapeDtypeStruct((HERE, 2, 3, NB, PDEV), BF16)
    return pl.pallas_call(
        modes_kernel,
        in_specs=[HELD] * (5 + 2 * TM),
        out_specs=[pl.BlockSpec(memory_space=pl.ANY)] * 2,
        out_shape=[gram, modes],
        scratch_shapes=[
            pltpu.VMEM(gram.shape, F32),
            pltpu.VMEM(modes.shape, BF16),
            pltpu.SemaphoreType.DMA((PAIRS + 1,)),
        ],
        compiler_params=pltpu.CompilerParams(vmem_limit_bytes=PART),
        cost_estimate=pl.CostEstimate(flops=0, bytes_accessed=0, transcendentals=0),
        name="modes",
    )(*totals, order, *pieces)


def over_space(block, mask):
    route = [(i, i ^ mask) for i in range(lax.axis_size("space"))]
    return lax.ppermute(block, "space", route)


def half_block_route():
    route = []
    for s in range(lax.axis_size("space")):
        for t in range(TM):
            if s % 2 == 1:
                route.append((s * TM + t, s * TM + (t + 1) % TM))
            elif t:
                route.append((s * TM + t, s * TM + t - 1))
    return route


def from_behind(block, distance):
    route = [(i, (i + distance) % TM) for i in range(TM)]
    return lax.ppermute(block, "tm", route)


def to_owners(pieces):
    far = from_behind(pieces[2], 2)
    return [pieces[0], from_behind(pieces[1], 1), far, from_behind(pieces[3], 3)]


def sum_over_space(terms):
    for shift in (4, 2, 0):
        got = [terms] + [over_space(terms, m << shift) for m in (1, 2, 3)]
        if shift:
            terms = (got[0] + got[1]) + (got[2] + got[3])
    return got


def body(snapshots, tail, volume):
    snaps = jnp.transpose(snapshots, (1, 0, 2))
    tail = jnp.transpose(tail, (1, 0, 2))
    weights = volume.reshape(1, PDEV)
    early_band, late_band = (jnp.asarray(b) for b in banded_tables())
    edge = lax.dynamic_slice_in_dim(snaps, core() * (OWN - 1) * HOP, HOP, 1)
    moved = lax.ppermute(edge, ("space", "tm"), half_block_route())
    blocks = [(snaps, BODY, 0), (snaps, HOP, HALF)]
    early = to_owners(transform(early_kernel, ALL, early_band, blocks, WHOLE))
    blocks = [(snaps, BODY, 1), (snaps, HOP, 0), (moved, HOP, 0), (tail, HOP, 0)]
    late = to_owners(transform(late_kernel, ALL, late_band, blocks, PART))
    pieces = early + late
    order = jnp.asarray(orders())
    terms = gram_terms(pieces, weights, order)
    gram, modes = project(sum_over_space(terms), order, pieces)
    return gram, jnp.transpose(modes, (0, 1, 3, 2, 4))


def solution(mesh):
    placed = (P("tm", None, "space"), P(None, None, "space"), P("space"))
    return jax.shard_map(
        body,
        mesh=mesh,
        in_specs=placed,
        out_specs=(P("tm", None, None, None), P("tm", None, None, None, "space")),
        check_vma=False,
    )
```

```python
import functools

import jax
import jax.numpy as jnp
import ml_dtypes
import numpy as np
from jax import lax
from jax.experimental import pallas as pl
from jax.experimental.pallas import tpu as pltpu
from jax.sharding import PartitionSpec as P

NB = 32
NFFT = 128
HOP = 64
SLOTS = 64
PDEV = 768
NPOINTS = 49152
TM = 4
OWN = NB // TM
HALF = OWN // 2
HERE = SLOTS // TM
BODY = HALF * HOP
ALL = (0, HERE // 2)
PAIRS, QUADS = HERE // 2, HERE // 4
PARTS = ((0, 3), (3, QUADS))
LONG = 10**12
F32, BF16 = jnp.float32, jnp.bfloat16
HELD = pl.BlockSpec(memory_space=pltpu.VMEM)
ANY = pl.BlockSpec(memory_space=pl.ANY)
WHOLE, PART = 60 << 20, 16 << 20


def transform_table():
    f32 = np.float32
    times = np.arange(NFFT, dtype=f32)
    freq = np.arange(SLOTS, dtype=f32)[:, None]
    window = f32(0.5) - f32(0.5) * np.cos(f32(2.0 * np.pi) * times / f32(NFFT))
    window = window / np.sqrt(np.sum(window * window))
    angles = f32(2.0 * np.pi) * freq * times[None, :] / f32(NFFT)
    real_rows = window * np.cos(angles)
    imag_rows = -window * np.sin(angles)
    nyquist = window * np.cos(f32(np.pi) * times)
    imag_rows = np.where(freq == 0, nyquist[None, :], imag_rows)
    return np.stack([real_rows, imag_rows], axis=1).astype(ml_dtypes.bfloat16)


def banded_tables():
    table = transform_table()

    def band(starts, span):
        rows = np.zeros((SLOTS, 2, HALF, span), ml_dtypes.bfloat16)
        for b, start in enumerate(starts):
            rows[:, :, b, start : start + NFFT] = table
        return rows.reshape(TM, HERE * 2 * HALF, span)

    starts = [b * HOP for b in range(HALF)]
    late = [band(starts, BODY + 2 * HOP), band(starts[:-1] + [BODY], BODY + 2 * HOP)]
    return band(starts, BODY + HOP), np.concatenate(late, 0)


def core():
    return lax.axis_index("space") % 2


def pick(flag, yes, no):
    chosen = jnp.full(yes.shape, flag.astype(jnp.int32), jnp.int32) > 0
    return jnp.where(chosen, yes.astype(F32), no.astype(F32)).astype(BF16)


def apply_band(pairs, band, base, main, after, outs):
    rank = lax.axis_index("tm")
    first, stop = (4 * HALF * p for p in pairs)
    rows = jnp.concatenate([band[base + (rank + k) % TM, first:stop] for k in range(TM)], 0)
    got = jnp.dot(rows[:, :BODY], main, preferred_element_type=F32)
    got += jnp.dot(rows[:, BODY:], after, preferred_element_type=F32)
    got = got.astype(BF16).reshape(TM, pairs[1] - pairs[0], 4 * HALF, PDEV)
    for k, out in enumerate(outs):
        out[:, 0] = got[k]


def early_kernel(pairs, band, main, after, *outs):
    apply_band(pairs, band, 0, main[0], after[0], outs)


def late_kernel(pairs, band, main, head, moved, tail, *outs):
    rank = lax.axis_index("tm")
    half = pick((rank == TM - 1) & (core() == 0), tail[0], moved[0])
    start = pick((rank == 0) & (core() == 1), tail[0], head[0])
    apply_band(pairs, band, TM * core(), main[0], jnp.concatenate([half, start], 0), outs)


def transform(kernel, pairs, band, blocks, limit):
    count = pairs[1] - pairs[0]

    def block(span, at):
        return pl.BlockSpec((1, span, PDEV), lambda c: (c, at, 0))

    return pl.pallas_call(
        functools.partial(kernel, pairs),
        grid=(3,),
        in_specs=[pl.BlockSpec(band.shape, lambda c: (0, 0, 0))]
        + [block(span, at) for _, span, at in blocks],
        out_specs=[pl.BlockSpec((count, 1, 4 * HALF, PDEV), lambda c: (0, c, 0, 0))] * TM,
        out_shape=[jax.ShapeDtypeStruct((count, 3, 4 * HALF, PDEV), BF16)] * TM,
        compiler_params=pltpu.CompilerParams(vmem_limit_bytes=limit),
        cost_estimate=pl.CostEstimate(flops=LONG, bytes_accessed=0, transcendentals=0),
        name="transform",
    )(band, *(array for array, _, _ in blocks))


def zero_lanes(is_first, lanes):
    return jnp.where((lax.axis_index("tm") == 0) & is_first, lanes, 0)


def lane_masks():
    lane = lax.broadcasted_iota(jnp.int32, (NB, 4 * NB), 1)
    return lane, lane < 2 * NB, (lane % (2 * NB)) < NB


def triangle():
    row = lax.broadcasted_iota(jnp.int32, (NB, 4 * NB), 0)
    return row, lax.broadcasted_iota(jnp.int32, (NB, 4 * NB), 1) % NB


def by_quarter(parts):
    lane, _, _ = lane_masks()
    out = parts[3]
    for at in (2, 1, 0):
        out = jnp.where(lane < (at + 1) * NB, parts[at], out)
    return out


def turn(x, quarters):
    return pltpu.roll(x, (quarters % 4) * NB, 1) if quarters % 4 else x


def transposed(four):
    flipped = jnp.concatenate([four] * 4, 0).T
    return by_quarter([flipped[g * NB : (g + 1) * NB] for g in range(4)])


def pair_terms(early, late, volume, spec, pair, is_first):
    rank = lax.axis_index("tm")
    row = lax.broadcasted_iota(jnp.int32, (OWN, PDEV), 0)
    upper = row < HALF
    moved = (row % HALF) >= jnp.where(core() == 1, HALF - 1, HALF)
    weights = volume[...]
    total = jnp.zeros((4 * NB, 4 * NB), F32)
    for c in range(3):
        rows = []
        for s in range(2):
            half = slice(s * OWN, (s + 1) * OWN)
            real, imag = [], []
            for q in range(TM):
                a = early[q, pair, c].astype(F32)[half]
                b = late[q, pair, c].astype(F32)[half]
                after = late[(q + 1) % TM, pair, c].astype(F32)[half]
                b = jnp.where(moved, after, b)
                real.append(jnp.where(upper, a, pltpu.roll(b, HALF, 0)))
                imag.append(jnp.where(upper, pltpu.roll(a, HALF, 0), b))
            rows += real + imag
        both = jnp.concatenate(rows, 0)
        plain = both.astype(BF16)
        weighted = (both * weights).astype(BF16)
        spec[pair, c] = plain
        total += lax.dot_general(
            weighted, plain, (((1,), (1,)), ((), ())), preferred_element_type=F32
        )
    lane, first, low = lane_masks()
    top = jnp.where(first, total[:NB], total[2 * NB : 3 * NB])
    bottom = jnp.where(first, total[NB : 2 * NB], total[3 * NB :])
    summed = top + jnp.where(low, turn(bottom, 3), 0.0)
    if pair:
        return summed
    apart = jnp.where(lane < NB, top, bottom)
    return jnp.where(lane < zero_lanes(is_first, 2 * NB), apart, summed)


def gram_kernel(quads, *refs):
    pieces, volume = refs[: 2 * TM], refs[2 * TM]
    terms, spec, early, late = refs[-4:]
    step = pl.program_id(0)
    rank = lax.axis_index("tm")
    for k in range(TM):
        early[(rank + TM - k) % TM] = pieces[k][...]
        late[(rank + TM - k) % TM] = pieces[TM + k][...]

    is_first = step + quads[0] == 0
    if quads[0]:

        @pl.when(step == 0)
        def _():
            terms[...] = refs[2 * TM + 1][...]

    one, two = (pair_terms(early, late, volume, spec, p, is_first) for p in range(2))
    sums = by_quarter([one, turn(one, -1), turn(two, 2), turn(two, 1)])
    cross = by_quarter([turn(one, -1), turn(one, -2), turn(two, 1), two])
    lane, _, _ = lane_masks()
    zero = lane < zero_lanes(is_first, NB)
    row, column = triangle()
    below = jnp.where(zero, cross, cross - transposed(cross))
    at = pl.multiple_of((step + quads[0]) * NB, NB)
    terms[pl.ds(at, NB)] = jnp.where(row <= column, sums, below)
    if not quads[0]:

        @pl.when(step == 0)
        def _():
            diagonal = jnp.sum(jnp.where(row == column, cross, 0.0), 0, keepdims=True)
            terms[QUADS * NB :] = jnp.broadcast_to(diagonal, (8, 4 * NB))


def gram_terms(quads, early, late, volume, before=(), cost=0):
    count, skip = quads[1] - quads[0], quads[0]
    block = (2, 3, 4 * HALF, PDEV)
    whole = ((QUADS * NB + 8), 4 * NB)
    return pl.pallas_call(
        functools.partial(gram_kernel, quads),
        grid=(count,),
        in_specs=[pl.BlockSpec(block, lambda p: (p + skip, 0, 0, 0))] * TM
        + [pl.BlockSpec(block, lambda p: (p, 0, 0, 0))] * TM
        + [pl.BlockSpec((1, PDEV), lambda p: (0, 0))]
        + [pl.BlockSpec(whole, lambda p: (0, 0)), ANY][: len(before)],
        out_specs=[
            pl.BlockSpec(whole, lambda p: (0, 0)),
            pl.BlockSpec((2, 3, 4 * NB, PDEV), lambda p: (p + skip, 0, 0, 0)),
        ],
        out_shape=[
            jax.ShapeDtypeStruct(whole, F32),
            jax.ShapeDtypeStruct((2 * QUADS, 3, 4 * NB, PDEV), BF16),
        ],
        scratch_shapes=[pltpu.VMEM((TM,) + block, BF16)] * 2,
        input_output_aliases={2 * TM + 2: 1} if before else {},
        compiler_params=pltpu.CompilerParams(vmem_limit_bytes=PART),
        cost_estimate=pl.CostEstimate(flops=cost, bytes_accessed=0, transcendentals=0),
        name="gram_terms",
    )(*early, *late, volume, *before)


def mix(mat, is_first):
    lane, first, low = lane_masks()
    zero = lane < (zero_lanes(True, 2 * NB) if is_first else 0)
    squares = mat * mat

    def part_sum(keep):
        return jnp.sum(jnp.where(keep, squares, 0.0), keepdims=True)

    e0, e1 = part_sum(lane < NB), part_sum(first & ~low)
    rest_sum = part_sum(~first)
    zero_here = zero[:1, :1]
    norm_a = jnp.sqrt(jnp.where(zero_here, e0, e0 + e1) + 1e-06)
    norm_b = jnp.sqrt(jnp.where(zero_here, e1, e0 + e1) + 1e-06)
    norm_rest = jnp.sqrt(rest_sum + 1e-06)
    turned = jnp.where(low, -turn(mat, 3), turn(mat, 1))
    part_a = jnp.where(zero, jnp.where(low, mat, 0.0), mat)
    part_b = jnp.where(zero, jnp.where(low, 0.0, mat), turned)
    part_a = part_a / jnp.where(first, norm_a, norm_rest)
    part_b = part_b / jnp.where(first, norm_b, norm_rest)
    mixing = jnp.concatenate(
        [
            jnp.where(first, part_a, 0.0),
            jnp.where(first, part_b, 0.0),
            jnp.where(first, 0.0, part_a),
            jnp.where(first, 0.0, part_b),
        ],
        0,
    )
    return mixing.astype(BF16)


def modes_kernel(t0, t1, t2, t3, spec, gram_out, modes_out, gram, modes, sems):
    total = ((t0[...] + t1[...]) + (t2[...] + t3[...])) / (NB * 3 * NPOINTS)
    row, column = triangle()
    lane, _, _ = lane_masks()
    mats = []
    for u in range(QUADS):
        packed = total[u * NB : (u + 1) * NB]
        other = transposed(packed)
        even = jnp.where(row <= column, packed, other)
        odd = jnp.where(row > column, packed, jnp.where(row < column, -other, 0.0))
        if u == 0:
            diagonal = total[QUADS * NB : QUADS * NB + 1]
            alone = jnp.where(row < column, other, jnp.where(row > column, packed, diagonal))
            odd = jnp.where(lane < zero_lanes(True, NB), alone, odd)
        mats.append(by_quarter([even, turn(odd, 1), turn(even, 1), turn(odd, 2)]))
        mats.append(by_quarter([turn(even, 2), turn(odd, -1), turn(even, -1), odd]))
    mixings = [mix(mat, pair == 0) for pair, mat in enumerate(mats)]
    copies = []
    for pair in range(PAIRS):
        slots = pl.ds(2 * pair, 2)
        for c in range(3):
            got = jnp.dot(mixings[pair], spec[pair, c], preferred_element_type=F32)
            modes[slots, :, c] = got.astype(BF16).reshape(2, 2, NB, PDEV)
        copies.append(pltpu.make_async_copy(modes.at[slots], modes_out.at[slots], sems.at[pair]))
        copies[-1].start()
    for pair, mat in enumerate(mats):
        for s in range(2):
            for part in range(2):
                at = (2 * s + part) * NB
                gram[2 * pair + s, part] = mat[:, at : at + NB]
    copies.append(pltpu.make_async_copy(gram, gram_out, sems.at[PAIRS]))
    copies[-1].start()
    for copy in copies:
        copy.wait()


def project(totals, spec):
    gram = jax.ShapeDtypeStruct((HERE, 2, NB, NB), F32)
    modes = jax.ShapeDtypeStruct((HERE, 2, 3, NB, PDEV), BF16)
    return pl.pallas_call(
        modes_kernel,
        in_specs=[HELD] * 5,
        out_specs=[pl.BlockSpec(memory_space=pl.ANY)] * 2,
        out_shape=[gram, modes],
        scratch_shapes=[
            pltpu.VMEM(gram.shape, F32),
            pltpu.VMEM(modes.shape, BF16),
            pltpu.SemaphoreType.DMA((PAIRS + 1,)),
        ],
        compiler_params=pltpu.CompilerParams(vmem_limit_bytes=PART),
        cost_estimate=pl.CostEstimate(flops=0, bytes_accessed=0, transcendentals=0),
        name="modes",
    )(*totals, spec)


def over_space(block, mask):
    route = [(i, i ^ mask) for i in range(lax.axis_size("space"))]
    return lax.ppermute(block, "space", route)


def half_block_route():
    route = []
    for s in range(lax.axis_size("space")):
        for t in range(TM):
            if s % 2 == 1:
                route.append((s * TM + t, s * TM + (t + 1) % TM))
            elif t:
                route.append((s * TM + t, s * TM + t - 1))
    return route


def from_behind(block, distance):
    route = [(i, (i + distance) % TM) for i in range(TM)]
    return lax.ppermute(block, "tm", route)


def to_owners(pieces):
    far = from_behind(pieces[2], 2)
    return [pieces[0], from_behind(pieces[1], 1), far, from_behind(pieces[3], 3)]


def sum_over_space(terms):
    for shift in (4, 2, 0):
        got = [terms] + [over_space(terms, m << shift) for m in (1, 2, 3)]
        if shift:
            terms = (got[0] + got[1]) + (got[2] + got[3])
    return got


def body(snapshots, tail, volume):
    snaps = jnp.transpose(snapshots, (1, 0, 2))
    tail = jnp.transpose(tail, (1, 0, 2))
    weights = volume.reshape(1, PDEV)
    early_band, late_band = (jnp.asarray(b) for b in banded_tables())
    edge = lax.dynamic_slice_in_dim(snaps, core() * (OWN - 1) * HOP, HOP, 1)
    moved = lax.ppermute(edge, ("space", "tm"), half_block_route())
    blocks = [(snaps, BODY, 0), (snaps, HOP, HALF)]
    early = to_owners(transform(early_kernel, ALL, early_band, blocks, WHOLE))
    blocks = [(snaps, BODY, 1), (snaps, HOP, 0), (moved, HOP, 0), (tail, HOP, 0)]
    late = [transform(late_kernel, (2 * a, 2 * b), late_band, blocks, PART) for a, b in PARTS]
    late = [to_owners(pieces) for pieces in late]
    sums = gram_terms(PARTS[0], early, late[0], weights, cost=LONG)
    terms, spec = gram_terms(PARTS[1], early, late[1], weights, sums)
    gram, modes = project(sum_over_space(terms), spec)
    return gram, jnp.transpose(modes, (0, 1, 3, 2, 4))


def solution(mesh):
    placed = (P("tm", None, "space"), P(None, None, "space"), P("space"))
    return jax.shard_map(
        body,
        mesh=mesh,
        in_specs=placed,
        out_specs=(P("tm", None, None, None), P("tm", None, None, None, "space")),
        check_vma=False,
    )
```

```python
import functools

import jax
import jax.numpy as jnp
import ml_dtypes
import numpy as np
from jax import lax
from jax.experimental import pallas as pl
from jax.experimental.pallas import tpu as pltpu
from jax.sharding import PartitionSpec as P

NB = 32
NFFT = 128
HOP = 64
SLOTS = 64
PDEV = 768
NPOINTS = 49152
TM = 4
OWN = NB // TM
HALF = OWN // 2
HERE = SLOTS // TM
BODY = HALF * HOP
ALL = (0, HERE // 2)
PAIRS, QUADS = HERE // 2, HERE // 4
PARTS = ((0, 3), (3, QUADS))
LONG = 10**12
F32, BF16 = jnp.float32, jnp.bfloat16
HELD = pl.BlockSpec(memory_space=pltpu.VMEM)
ANY = pl.BlockSpec(memory_space=pl.ANY)
WHOLE, PART = 60 << 20, 16 << 20


def transform_table():
    f32 = np.float32
    times = np.arange(NFFT, dtype=f32)
    freq = np.arange(SLOTS, dtype=f32)[:, None]
    window = f32(0.5) - f32(0.5) * np.cos(f32(2.0 * np.pi) * times / f32(NFFT))
    window = window / np.sqrt(np.sum(window * window))
    angles = f32(2.0 * np.pi) * freq * times[None, :] / f32(NFFT)
    real_rows = window * np.cos(angles)
    imag_rows = -window * np.sin(angles)
    nyquist = window * np.cos(f32(np.pi) * times)
    imag_rows = np.where(freq == 0, nyquist[None, :], imag_rows)
    return np.stack([real_rows, imag_rows], axis=1).astype(ml_dtypes.bfloat16)


def banded_tables():
    table = transform_table()

    def band(starts, span):
        rows = np.zeros((SLOTS, 2, HALF, span), ml_dtypes.bfloat16)
        for b, start in enumerate(starts):
            rows[:, :, b, start : start + NFFT] = table
        return rows.reshape(TM, HERE * 2 * HALF, span)

    starts = [b * HOP for b in range(HALF)]
    late = [band(starts, BODY + 2 * HOP), band(starts[:-1] + [BODY], BODY + 2 * HOP)]
    return band(starts, BODY + HOP), np.concatenate(late, 0)


def core():
    return lax.axis_index("space") % 2


def pick(flag, yes, no):
    chosen = jnp.full(yes.shape, flag.astype(jnp.int32), jnp.int32) > 0
    return jnp.where(chosen, yes.astype(F32), no.astype(F32)).astype(BF16)


def apply_band(pairs, band, base, main, after, outs):
    rank = lax.axis_index("tm")
    first, stop = (4 * HALF * p for p in pairs)
    rows = jnp.concatenate([band[base + (rank + k) % TM, first:stop] for k in range(TM)], 0)
    got = jnp.dot(rows[:, :BODY], main, preferred_element_type=F32)
    got += jnp.dot(rows[:, BODY:], after, preferred_element_type=F32)
    got = got.astype(BF16).reshape(TM, pairs[1] - pairs[0], 4 * HALF, PDEV)
    for k, out in enumerate(outs):
        out[:, 0] = got[k]


def early_kernel(pairs, band, main, after, *outs):
    apply_band(pairs, band, 0, main[0], after[0], outs)


def late_kernel(pairs, band, main, head, moved, tail, *outs):
    rank = lax.axis_index("tm")
    half = pick((rank == TM - 1) & (core() == 0), tail[0], moved[0])
    start = pick((rank == 0) & (core() == 1), tail[0], head[0])
    apply_band(pairs, band, TM * core(), main[0], jnp.concatenate([half, start], 0), outs)


def transform(kernel, pairs, band, blocks, limit):
    count = pairs[1] - pairs[0]

    def block(span, at):
        return pl.BlockSpec((1, span, PDEV), lambda c: (c, at, 0))

    return pl.pallas_call(
        functools.partial(kernel, pairs),
        grid=(3,),
        in_specs=[pl.BlockSpec(band.shape, lambda c: (0, 0, 0))]
        + [block(span, at) for _, span, at in blocks],
        out_specs=[pl.BlockSpec((count, 1, 4 * HALF, PDEV), lambda c: (0, c, 0, 0))] * TM,
        out_shape=[jax.ShapeDtypeStruct((count, 3, 4 * HALF, PDEV), BF16)] * TM,
        compiler_params=pltpu.CompilerParams(vmem_limit_bytes=limit),
        cost_estimate=pl.CostEstimate(flops=LONG, bytes_accessed=0, transcendentals=0),
        name="transform",
    )(band, *(array for array, _, _ in blocks))


def zero_lanes(is_first, lanes):
    return jnp.where((lax.axis_index("tm") == 0) & is_first, lanes, 0)


def lane_masks():
    lane = lax.broadcasted_iota(jnp.int32, (NB, 4 * NB), 1)
    return lane, lane < 2 * NB, (lane % (2 * NB)) < NB


def triangle():
    row = lax.broadcasted_iota(jnp.int32, (NB, 4 * NB), 0)
    return row, lax.broadcasted_iota(jnp.int32, (NB, 4 * NB), 1) % NB


def by_quarter(parts):
    lane, _, _ = lane_masks()
    out = parts[3]
    for at in (2, 1, 0):
        out = jnp.where(lane < (at + 1) * NB, parts[at], out)
    return out


def turn(x, quarters):
    return pltpu.roll(x, (quarters % 4) * NB, 1) if quarters % 4 else x


def transposed(four):
    flipped = jnp.concatenate([four] * 4, 0).T
    return by_quarter([flipped[g * NB : (g + 1) * NB] for g in range(4)])


def pair_terms(early, late, volume, spec, pair, is_first):
    rank = lax.axis_index("tm")
    row = lax.broadcasted_iota(jnp.int32, (OWN, PDEV), 0)
    upper = row < HALF
    moved = (row % HALF) >= jnp.where(core() == 1, HALF - 1, HALF)
    weights = volume[...]
    total = jnp.zeros((4 * NB, 4 * NB), F32)
    for c in range(3):
        rows = []
        for s in range(2):
            half = slice(s * OWN, (s + 1) * OWN)
            real, imag = [], []
            for q in range(TM):
                a = early[q, pair, c].astype(F32)[half]
                b = late[q, pair, c].astype(F32)[half]
                after = late[(q + 1) % TM, pair, c].astype(F32)[half]
                b = jnp.where(moved, after, b)
                real.append(jnp.where(upper, a, pltpu.roll(b, HALF, 0)))
                imag.append(jnp.where(upper, pltpu.roll(a, HALF, 0), b))
            rows += real + imag
        both = jnp.concatenate(rows, 0)
        plain = both.astype(BF16)
        weighted = (both * weights).astype(BF16)
        spec[pair, c] = plain
        total += lax.dot_general(
            weighted, plain, (((1,), (1,)), ((), ())), preferred_element_type=F32
        )
    lane, first, low = lane_masks()
    top = jnp.where(first, total[:NB], total[2 * NB : 3 * NB])
    bottom = jnp.where(first, total[NB : 2 * NB], total[3 * NB :])
    summed = top + jnp.where(low, turn(bottom, 3), 0.0)
    if pair:
        return summed
    apart = jnp.where(lane < NB, top, bottom)
    return jnp.where(lane < zero_lanes(is_first, 2 * NB), apart, summed)


def gram_kernel(quads, *refs):
    pieces, volume = refs[: 2 * TM], refs[2 * TM]
    terms, spec, early, late = refs[-4:]
    step = pl.program_id(0)
    rank = lax.axis_index("tm")
    for k in range(TM):
        early[(rank + TM - k) % TM] = pieces[k][...]
        late[(rank + TM - k) % TM] = pieces[TM + k][...]

    is_first = step + quads[0] == 0
    if quads[0]:

        @pl.when(step == 0)
        def _():
            terms[...] = refs[2 * TM + 1][...]

    one, two = (pair_terms(early, late, volume, spec, p, is_first) for p in range(2))
    sums = by_quarter([one, turn(one, -1), turn(two, 2), turn(two, 1)])
    cross = by_quarter([turn(one, -1), turn(one, -2), turn(two, 1), two])
    lane, _, _ = lane_masks()
    zero = lane < zero_lanes(is_first, NB)
    row, column = triangle()
    below = jnp.where(zero, cross, cross - transposed(cross))
    at = pl.multiple_of((step + quads[0]) * NB, NB)
    terms[pl.ds(at, NB)] = jnp.where(row <= column, sums, below)
    if not quads[0]:

        @pl.when(step == 0)
        def _():
            diagonal = jnp.sum(jnp.where(row == column, cross, 0.0), 0, keepdims=True)
            terms[QUADS * NB :] = jnp.broadcast_to(diagonal, (8, 4 * NB))


def gram_terms(quads, early, late, volume, before=(), cost=0):
    count, skip = quads[1] - quads[0], quads[0]
    block = (2, 3, 4 * HALF, PDEV)
    whole = ((QUADS * NB + 8), 4 * NB)
    return pl.pallas_call(
        functools.partial(gram_kernel, quads),
        grid=(count,),
        in_specs=[pl.BlockSpec(block, lambda p: (p + skip, 0, 0, 0))] * TM
        + [pl.BlockSpec(block, lambda p: (p, 0, 0, 0))] * TM
        + [pl.BlockSpec((1, PDEV), lambda p: (0, 0))]
        + [pl.BlockSpec(whole, lambda p: (0, 0)), ANY][: len(before)],
        out_specs=[
            pl.BlockSpec(whole, lambda p: (0, 0)),
            pl.BlockSpec((2, 3, 4 * NB, PDEV), lambda p: (p + skip, 0, 0, 0)),
        ],
        out_shape=[
            jax.ShapeDtypeStruct(whole, F32),
            jax.ShapeDtypeStruct((2 * QUADS, 3, 4 * NB, PDEV), BF16),
        ],
        scratch_shapes=[pltpu.VMEM((TM,) + block, BF16)] * 2,
        input_output_aliases={2 * TM + 2: 1} if before else {},
        compiler_params=pltpu.CompilerParams(vmem_limit_bytes=PART),
        cost_estimate=pl.CostEstimate(flops=cost, bytes_accessed=0, transcendentals=0),
        name="gram_terms",
    )(*early, *late, volume, *before)


def mix(mat, is_first):
    lane, first, low = lane_masks()
    zero = lane < (zero_lanes(True, 2 * NB) if is_first else 0)
    squares = mat * mat

    def part_sum(keep):
        return jnp.sum(jnp.where(keep, squares, 0.0), keepdims=True)

    e0, e1 = part_sum(lane < NB), part_sum(first & ~low)
    rest_sum = part_sum(~first)
    zero_here = zero[:1, :1]
    norm_a = jnp.sqrt(jnp.where(zero_here, e0, e0 + e1) + 1e-06)
    norm_b = jnp.sqrt(jnp.where(zero_here, e1, e0 + e1) + 1e-06)
    norm_rest = jnp.sqrt(rest_sum + 1e-06)
    turned = jnp.where(low, -turn(mat, 3), turn(mat, 1))
    part_a = jnp.where(zero, jnp.where(low, mat, 0.0), mat)
    part_b = jnp.where(zero, jnp.where(low, 0.0, mat), turned)
    part_a = part_a / jnp.where(first, norm_a, norm_rest)
    part_b = part_b / jnp.where(first, norm_b, norm_rest)
    mixing = jnp.concatenate(
        [
            jnp.where(first, part_a, 0.0),
            jnp.where(first, part_b, 0.0),
            jnp.where(first, 0.0, part_a),
            jnp.where(first, 0.0, part_b),
        ],
        0,
    )
    return mixing.astype(BF16)


def modes_kernel(t0, t1, t2, t3, spec, gram_out, modes_out, gram, modes, sems):
    total = ((t0[...] + t1[...]) + (t2[...] + t3[...])) / (NB * 3 * NPOINTS)
    row, column = triangle()
    lane, _, _ = lane_masks()
    mats = []
    for u in range(QUADS):
        packed = total[u * NB : (u + 1) * NB]
        other = transposed(packed)
        even = jnp.where(row <= column, packed, other)
        odd = jnp.where(row > column, packed, jnp.where(row < column, -other, 0.0))
        if u == 0:
            diagonal = total[QUADS * NB : QUADS * NB + 1]
            alone = jnp.where(row < column, other, jnp.where(row > column, packed, diagonal))
            odd = jnp.where(lane < zero_lanes(True, NB), alone, odd)
        mats.append(by_quarter([even, turn(odd, 1), turn(even, 1), turn(odd, 2)]))
        mats.append(by_quarter([turn(even, 2), turn(odd, -1), turn(even, -1), odd]))
    mixings = [mix(mat, pair == 0) for pair, mat in enumerate(mats)]
    copies = []
    for pair in range(PAIRS):
        slots = pl.ds(2 * pair, 2)
        for c in range(3):
            got = jnp.dot(mixings[pair], spec[pair, c], preferred_element_type=F32)
            modes[slots, :, c] = got.astype(BF16).reshape(2, 2, NB, PDEV)
        copies.append(pltpu.make_async_copy(modes.at[slots], modes_out.at[slots], sems.at[pair]))
        copies[-1].start()
    for pair, mat in enumerate(mats):
        for s in range(2):
            for part in range(2):
                at = (2 * s + part) * NB
                gram[2 * pair + s, part] = mat[:, at : at + NB]
    copies.append(pltpu.make_async_copy(gram, gram_out, sems.at[PAIRS]))
    copies[-1].start()
    for copy in copies:
        copy.wait()


def project(totals, spec):
    gram = jax.ShapeDtypeStruct((HERE, 2, NB, NB), F32)
    modes = jax.ShapeDtypeStruct((HERE, 2, 3, NB, PDEV), BF16)
    return pl.pallas_call(
        modes_kernel,
        in_specs=[HELD] * 5,
        out_specs=[pl.BlockSpec(memory_space=pl.ANY)] * 2,
        out_shape=[gram, modes],
        scratch_shapes=[
            pltpu.VMEM(gram.shape, F32),
            pltpu.VMEM(modes.shape, BF16),
            pltpu.SemaphoreType.DMA((PAIRS + 1,)),
        ],
        compiler_params=pltpu.CompilerParams(vmem_limit_bytes=PART),
        cost_estimate=pl.CostEstimate(flops=0, bytes_accessed=0, transcendentals=0),
        name="modes",
    )(*totals, spec)


def over_space(block, mask):
    route = [(i, i ^ mask) for i in range(lax.axis_size("space"))]
    return lax.ppermute(block, "space", route)


def half_block_route():
    route = []
    for s in range(lax.axis_size("space")):
        for t in range(TM):
            if s % 2 == 1:
                route.append((s * TM + t, s * TM + (t + 1) % TM))
            elif t:
                route.append((s * TM + t, s * TM + t - 1))
    return route


def from_behind(block, distance):
    route = [(i, (i + distance) % TM) for i in range(TM)]
    return lax.ppermute(block, "tm", route)


def to_owners(pieces):
    far = from_behind(pieces[2], 2)
    return [pieces[0], from_behind(pieces[1], 1), far, from_behind(pieces[3], 3)]


def sum_over_space(terms):
    for first, second in ((1, 2), (16, 32), (4, 8)):
        got = [terms] + [over_space(terms, m) for m in (first, second, first ^ second)]
        if (first, second) != (4, 8):
            terms = (got[0] + got[1]) + (got[2] + got[3])
    return got


def body(snapshots, tail, volume):
    snaps = jnp.transpose(snapshots, (1, 0, 2))
    tail = jnp.transpose(tail, (1, 0, 2))
    weights = volume.reshape(1, PDEV)
    early_band, late_band = (jnp.asarray(b) for b in banded_tables())
    edge = lax.dynamic_slice_in_dim(snaps, core() * (OWN - 1) * HOP, HOP, 1)
    moved = lax.ppermute(edge, ("space", "tm"), half_block_route())
    blocks = [(snaps, BODY, 0), (snaps, HOP, HALF)]
    early = to_owners(transform(early_kernel, ALL, early_band, blocks, WHOLE))
    blocks = [(snaps, BODY, 1), (snaps, HOP, 0), (moved, HOP, 0), (tail, HOP, 0)]
    late = [transform(late_kernel, (2 * a, 2 * b), late_band, blocks, PART) for a, b in PARTS]
    late = [to_owners(pieces) for pieces in late]
    sums = gram_terms(PARTS[0], early, late[0], weights, cost=LONG)
    terms, spec = gram_terms(PARTS[1], early, late[1], weights, sums)
    gram, modes = project(sum_over_space(terms), spec)
    return gram, jnp.transpose(modes, (0, 1, 3, 2, 4))


def solution(mesh):
    placed = (P("tm", None, "space"), P(None, None, "space"), P("space"))
    return jax.shard_map(
        body,
        mesh=mesh,
        in_specs=placed,
        out_specs=(P("tm", None, None, None), P("tm", None, None, None, "space")),
        check_vma=False,
    )
```
